256 devices in a mesh: grp: 4 (over y), row: 16 (over z_lo, x), col: 4 (over z_hi, core).
Axes of the slice: x: 4, y: 4, z: 8 (z_hi: 2, z_lo: 4; z = z_hi * 4 + z_lo), core: 2. Of those that a mesh axis runs over, the one named last changes fastest.
Arguments:
- teacher_in: bfloat16 [2048, 12288], P(('grp', 'col'), 'row'), may hold values from -6 to 6
- weight: bfloat16 [12288, 12288], P('row', ('grp', 'col')), may hold values from -0.0546875 to 0.0546875
- student_in: bfloat16 [2048, 12288], P(('grp', 'col'), 'row'), may hold values from -6 to 6
- kept_blocks: int32 [48], replicated, may hold values from 0 to 95, as said below
Outputs:
- gram_tile: float32 [6144, 6144], P('row', ('grp', 'col'))
- cross_tile: float32 [6144, 12288], P('row', ('grp', 'col'))
The draws below stay inside these ranges and needn't reach their ends.
Inputs may be any that keep to these rules, and one draw needn't show every extreme that they name: `kept_blocks`: distinct, in rising order; the first and the last block are always kept.
All inputs are finite; a program needn't handle non-finite values.
Results may differ from the reference program's by a relative error of at most 0.0029.
Values may be sent and summed in bfloat16 or wider, within the bound.
A program may use at most 64 MiB of HBM per device.

```python
import jax
import jax.numpy as jnp
from jax import lax

D = 12288
BLOCK = 128
KEPT_BLOCKS = 48
NB = 96
TOKENS = 2048


def draw_kept_blocks(key, part):
    key = jax.random.fold_in(key, 7)
    middle = jax.random.permutation(key, NB - 2).astype(jnp.int32) + 1
    chosen = middle[:KEPT_BLOCKS - 2]
    ends = jnp.array([0, NB - 1], dtype=jnp.int32)
    return jnp.sort(jnp.concatenate([ends, chosen])).astype(jnp.int32)


def block_scale(stream_key, shape, cuts, smallest, high):
    def one(dim, parts):
        steps = jax.random.uniform(jax.random.fold_in(jax.random.fold_in(stream_key, 6), dim), (parts,), jnp.float32, smallest / len(cuts), high / len(cuts))
        return jnp.repeat(jnp.exp(steps), shape[dim] // parts).reshape((-1,) + (1,) * (len(shape) - dim - 1))

    gain = one(*cuts[0])
    for cut in cuts[1:]:
        gain = gain * one(*cut)
    return gain


def scatter_about(own_key, extent, scale, most, split=(), kind=jnp.bfloat16):
    loudness = block_scale(own_key, extent, split, -0.22, 0.18) if split else 1.0
    drawn = jax.random.normal(own_key, extent, jnp.float32) * scale * loudness
    return jnp.minimum(jnp.maximum(drawn, -most), most).astype(kind)


def setup_inputs(seed: int = 0) -> dict:
    key_of = jax.random.split(jax.random.key(seed), 5)
    teacher_in = scatter_about(key_of[0], (TOKENS, D), 1.0, 6.0, ((0, 16), (1, 16)))
    weight = scatter_about(key_of[1], (D, D), D ** -0.5, 0.0546875, ((0, 16), (1, 16)))
    student_in = scatter_about(key_of[2], (TOKENS, D), 1.0, 6.0, ((0, 16), (1, 16)))
    kept_blocks = draw_kept_blocks(jax.random.fold_in(key_of[4], 71), 0)
    return {"teacher_in": teacher_in, "weight": weight, "student_in": student_in, "kept_blocks": kept_blocks}


def reference(teacher_in, weight, student_in, kept_blocks):
    teacher_out = jnp.dot(teacher_in, weight, preferred_element_type=jnp.float32).astype(jnp.bfloat16)
    offsets = jnp.arange(BLOCK, dtype=jnp.int32)
    columns = (kept_blocks[:, None] * BLOCK + offsets[None, :]).reshape(-1).astype(jnp.int32)
    kept_data = jnp.take(student_in, columns, axis=1)
    inv_count = 1.0 / TOKENS
    dims = (((0,), (0,)), ((), ()))
    gram_tile = lax.dot_general(kept_data, kept_data, dims, preferred_element_type=jnp.float32) * inv_count
    cross_tile = lax.dot_general(kept_data, teacher_out, dims, preferred_element_type=jnp.float32) * inv_count
    return gram_tile, cross_tile
```

```python
import jax
import jax.numpy as jnp
from jax import lax
from jax.experimental import pallas as pl
from jax.experimental.pallas import tpu as pltpu
from jax.sharding import PartitionSpec as P

MESH = pl.DeviceIdType.MESH
F32 = jnp.float32
BF16 = jnp.bfloat16
RING = 4
TOK = 128
PIECE = TOK // RING
FEAT = 768
KEPT = 384
BLOCK = 128
SLOTS = KEPT // BLOCK
ZBLOCKS = RING * FEAT // BLOCK
ORDER = (0, 1, 3, 2)
INV = 1.0 / 2048
COPIES = 120


def wrap(v):
    return lax.rem(v + RING, RING)


def kernel(kept, x_ref, w_ref, s_ref, gram_ref, cross_ref,
           xg, part, xin, total, zin, tg, sg, pack, kin, tile, kr, kc,
           send_sem, recv_sem):
    y, row, col = lax.axis_index("grp"), lax.axis_index("row"), lax.axis_index("col")
    zl, x = lax.div(row, RING), lax.rem(row, RING)
    core = lax.rem(col, 2)
    sib = col + 1 - 2 * core
    far = wrap(col + 2)
    far_sib = wrap(sib + 2)

    def to_x(k):
        return (y, zl * RING + wrap(x + k), col)

    def to_y(k):
        return (wrap(y + k), row, col)

    def to_z(k):
        return (y, wrap(zl + k) * RING + x, col)

    to_far = (y, row, far)
    to_sib = (y, row, sib)
    flip = (zl, y * RING + col, x)
    off_diagonal = row != y * RING + col

    count = [0]
    sent = []

    def copy(src, dst, device):
        i = count[0]
        count[0] += 1
        return pltpu.make_async_remote_copy(
            src_ref=src, dst_ref=dst, send_sem=send_sem.at[i], recv_sem=recv_sem.at[i],
            device_id=device, device_id_type=MESH)

    def push(src, dst, device):
        c = copy(src, dst, device)
        c.start()
        sent.append(c)
        return c

    kin[...] = jnp.zeros_like(kin)
    barrier = pltpu.get_barrier_semaphore()
    peers = [to_far, to_sib] + [f(k) for f in (to_x, to_y, to_z) for k in (1, 2, 3)]
    for p in peers:
        pl.semaphore_signal(barrier, inc=1, device_id=p, device_id_type=MESH)

    @pl.when(off_diagonal)
    def _():
        pl.semaphore_signal(barrier, inc=1, device_id=flip, device_id_type=MESH)

    pl.semaphore_wait(barrier, len(peers) + off_diagonal.astype(jnp.int32))

    class Gather:
        def __init__(self, buf, own):
            self.buf = buf
            self.far = push(own, buf.at[y, col], to_far)
            self.sib = {(0, 0): push(own, buf.at[y, col], to_sib)}
            self.near = {(k, 0): push(own, buf.at[y, col], to_y(k)) for k in ORDER[1:]}
            buf[y, col] = own[...]

        def spread(self):
            self.far.wait_recv()
            piece = self.buf.at[y, far]
            self.sib[0, 1] = push(piece, piece, to_sib)
            for k in ORDER[1:]:
                self.near[k, 1] = push(piece, piece, to_y(k))

        def hand(self, k):
            for w, c in ((0, col), (1, far)):
                self.near[k, w].wait_recv()
                piece = self.buf.at[wrap(y - k), c]
                self.sib[k, w] = push(piece, piece, to_sib)

        def ready(self, k):
            for w in (0, 1):
                self.sib[k, w].wait_recv()

    gx = Gather(xg, x_ref)

    for b in range(FEAT // BLOCK):
        sg[x * 6 + b] = s_ref[:, b * BLOCK:(b + 1) * BLOCK]
    own_blocks = sg.at[pl.ds(x * 6, 6)]
    student = [push(own_blocks, own_blocks, to_x(k)) for k in (1, 3, 2)]

    rsx, rsz, agz, agx, fwd = {}, {}, {}, {}, {}
    quarter = [wrap(y - k) for k in ORDER]

    def stage_a(i):
        q = quarter[i]

        def body(h, carry):
            lhs = xg[q, pl.ds(2 * h, 2)].reshape(2 * TOK, FEAT)
            out = jnp.dot(lhs, w_ref[...], preferred_element_type=F32)
            part[i, 2 * h] = out[:TOK].astype(BF16)
            part[i, 2 * h + 1] = out[TOK:].astype(BF16)

            @pl.when(x == 2 * h)
            def _():
                total[i] = out[:TOK]

            @pl.when(x == 2 * h + 1)
            def _():
                total[i] = out[TOK:]

            return carry

        lax.fori_loop(0, 2, body, 0)
        for n, k in enumerate((1, 3, 2)):
            rsx[i, n] = push(part.at[i, wrap(x + k)], xin.at[i, n], to_x(k))

    def stage_b(i):
        for n in range(3):
            rsx[i, n].wait_recv()
        total[i] = (total[i] + xin[i, 0].astype(F32)) + (xin[i, 1].astype(F32) + xin[i, 2].astype(F32))
        for n, k in enumerate((1, 2, 3)):
            rsz[i, n] = push(total.at[i, pl.ds(wrap(zl + k) * PIECE, PIECE)], zin.at[i, n], to_z(k))

    def stage_c(i):
        for n in range(3):
            rsz[i, n].wait_recv()
        mine = pl.ds(zl * PIECE, PIECE)
        tg[quarter[i], x, mine] = ((total[i, mine] + zin[i, 0]) + (zin[i, 1] + zin[i, 2])).astype(BF16)
        piece = tg.at[quarter[i], x, mine]
        for k in (1, 2, 3):
            agz[i, k] = push(piece, piece, to_z(k))

    def stage_d(i):
        for k in (1, 2, 3):
            agz[i, k].wait_recv()
        piece = tg.at[quarter[i], x]
        for k in (1, 3):
            agx[i, k] = push(piece, piece, to_x(k))

    def stage_e(i):
        for k, lo in ((1, 0), (3, TOK // 2)):
            agx[i, k].wait_recv()
            piece = tg.at[quarter[i], wrap(x - k), pl.ds(lo, TOK // 2)]
            fwd[i, k] = push(piece, piece, to_x(k))

    def stage_f(i):
        for k in (1, 3):
            fwd[i, k].wait_recv()
        q = quarter[i]
        lhs = kr[q].reshape(RING * TOK, KEPT)
        rhs = tg[q].reshape(RING * TOK, FEAT)
        out = lax.dot_general(lhs, rhs, (((0,), (0,)), ((), ())), preferred_element_type=F32)
        if i == 0:
            cross_ref[...] = out
        elif i < 3:
            cross_ref[...] += out
        else:
            cross_ref[...] = (cross_ref[...] + out) * INV

    gx.spread()

    for c in student:
        c.wait_recv()

    def linked(src, dst):
        gap = dst - src
        return (gap == 1) | (gap == -1) | ((src == 2) & (dst == 0)) | ((src == 1) & (dst == 3))

    packs = []
    for k in range(RING):
        zt = wrap(zl + k)
        for j in range(SLOTS):
            at = kept[(zt * RING + x) * SLOTS + j] - zl * ZBLOCKS
            at = jnp.minimum(jnp.maximum(at, 0), ZBLOCKS - 1)
            if k == 0:
                kin[zl * SLOTS + j] = sg[at]
            else:
                pack[(k - 1) * SLOTS + j] = sg[at]
        if k:
            c = copy(pack.at[pl.ds((k - 1) * SLOTS, SLOTS)], kin.at[pl.ds(zl * SLOTS, SLOTS)], to_z(k))
            packs.append((k, c))

            @pl.when(linked(zl, zt))
            def _():
                c.start()

    gx.ready(0)
    stage_a(0)

    for k, c in packs:
        @pl.when(linked(wrap(zl - k), zl))
        def _():
            c.wait_recv()

    for j in range(SLOTS):
        at = kept[row * SLOTS + j]
        tile[:, j * BLOCK:(j + 1) * BLOCK] = kin[lax.div(at, ZBLOCKS) * SLOTS + j]
    gk = Gather(kr, tile)
    share = copy(tile, kc.at[col, y], flip)

    @pl.when(off_diagonal)
    def _():
        share.start()

    @pl.when(jnp.logical_not(off_diagonal))
    def _():
        kc[x, zl] = tile[...]

    gx.hand(ORDER[1])
    gx.ready(ORDER[1])
    stage_a(1)
    gk.spread()
    stage_b(0)

    gx.hand(ORDER[2])
    gx.ready(ORDER[2])
    stage_a(2)

    @pl.when(off_diagonal)
    def _():
        share.wait_recv()

    own_share = kc.at[x, zl]
    colz = [push(own_share, own_share, to_z(k)) for k in (1, 2, 3)]

    stage_b(1)
    stage_c(0)

    gx.hand(ORDER[3])
    gx.ready(ORDER[3])
    stage_a(3)

    for k in ORDER[1:]:
        gk.hand(k)
    stage_b(2)
    stage_c(1)
    stage_d(0)
    for c in colz:
        c.wait_recv()
    colx = {k: push(kc.at[x], kc.at[x], to_x(k)) for k in (1, 3)}
    stage_b(3)
    stage_c(2)
    stage_d(1)
    stage_e(0)
    for k in ORDER:
        gk.ready(k)
    stage_c(3)
    stage_d(2)
    stage_e(1)
    colf = {}
    for k, lo in ((1, 0), (3, 2)):
        colx[k].wait_recv()
        piece = kc.at[wrap(x - k), pl.ds(lo, 2)]
        colf[k] = push(piece, piece, to_x(k))
    stage_f(0)
    stage_d(3)
    stage_e(2)
    stage_f(1)
    for k in (1, 3):
        colf[k].wait_recv()

    def gram_body(j, carry):
        lhs = kr[:, j].reshape(RING * TOK, KEPT)
        rhs = kc[j].reshape(RING * TOK, KEPT)
        gram_ref[...] += lax.dot_general(lhs, rhs, (((0,), (0,)), ((), ())), preferred_element_type=F32)
        return carry

    gram_ref[...] = jnp.zeros_like(gram_ref)
    lax.fori_loop(0, RING, gram_body, 0)
    gram_ref[...] = gram_ref[...] * INV
    stage_e(3)
    stage_f(2)
    stage_f(3)

    for c in sent:
        c.wait_send()
    for k, c in packs:
        @pl.when(linked(zl, wrap(zl + k)))
        def _():
            c.wait_send()

    @pl.when(off_diagonal)
    def _():
        share.wait_send()


def local(teacher_in, weight, student_in, kept_blocks):
    vmem = pl.BlockSpec(memory_space=pltpu.VMEM)
    return pl.pallas_call(
        kernel,
        out_shape=(jax.ShapeDtypeStruct((KEPT, KEPT), F32),
                   jax.ShapeDtypeStruct((KEPT, FEAT), F32)),
        in_specs=[pl.BlockSpec(memory_space=pltpu.SMEM), vmem, vmem, vmem],
        out_specs=(vmem, vmem),
        scratch_shapes=[
            pltpu.VMEM((RING, RING, TOK, FEAT), BF16),
            pltpu.VMEM((RING, RING, TOK, FEAT), BF16),
            pltpu.VMEM((RING, 3, TOK, FEAT), BF16),
            pltpu.VMEM((RING, TOK, FEAT), F32),
            pltpu.VMEM((RING, 3, PIECE, FEAT), F32),
            pltpu.VMEM((RING, RING, TOK, FEAT), BF16),
            pltpu.VMEM((ZBLOCKS, TOK, BLOCK), BF16),
            pltpu.VMEM((3 * SLOTS, TOK, BLOCK), BF16),
            pltpu.VMEM((RING * SLOTS, TOK, BLOCK), BF16),
            pltpu.VMEM((TOK, KEPT), BF16),
            pltpu.VMEM((RING, RING, TOK, KEPT), BF16),
            pltpu.VMEM((RING, RING, TOK, KEPT), BF16),
            pltpu.SemaphoreType.DMA((COPIES,)),
            pltpu.SemaphoreType.DMA((COPIES,)),
        ],
        compiler_params=pltpu.CompilerParams(
            collective_id=0, has_side_effects=True, vmem_limit_bytes=48 << 20),
        name="gram_cross",
    )(kept_blocks, teacher_in, weight, student_in)


def solution(mesh):
    return jax.shard_map(
        local,
        mesh=mesh,
        in_specs=(
            P(("grp", "col"), "row"),
            P("row", ("grp", "col")),
            P(("grp", "col"), "row"),
            P(),
        ),
        out_specs=(P("row", ("grp", "col")), P("row", ("grp", "col"))),
        check_vma=False,
    )
```

```python
import jax
import jax.numpy as jnp
from jax import lax
from jax.experimental import pallas as pl
from jax.experimental.pallas import tpu as pltpu
from jax.sharding import PartitionSpec as P

MESH = pl.DeviceIdType.MESH
F32 = jnp.float32
BF16 = jnp.bfloat16
RING = 4
TOK = 128
PAIR = 2 * TOK
SUB = PAIR // RING
HALF = SUB // 2
FEAT = 768
KEPT = 384
BLOCK = 128
OWN = FEAT // BLOCK
SLOTS = KEPT // BLOCK
ORDER = (0, 1, 3, 2)
CHUNKS = tuple((k, w) for w in (0, 1) for k in ORDER)
INV = 1.0 / 2048
COPIES = 180


def wrap(v):
    return lax.rem(v + RING, RING)


def always(body):
    body()


def kernel(kept, x_hbm, w_hbm, s_hbm, gram_ref, cross_ref,
           xg, wv, sblk, part, mine, xin, total, zin, zhalf, tg,
           packx, sx, packz, kin, tile, kr, kc,
           load_sem, send_sem, recv_sem):
    y, row, col = lax.axis_index("grp"), lax.axis_index("row"), lax.axis_index("col")
    zl, x = lax.div(row, RING), lax.rem(row, RING)
    zh, core = lax.div(col, 2), lax.rem(col, 2)
    sib = col + 1 - 2 * core
    far = wrap(col + 2)
    inner = (zl == 1) | (zl == 2)
    outer = jnp.logical_not(inner)

    def to_x(k):
        return (y, zl * RING + wrap(x + k), col)

    def to_y(k):
        return (wrap(y + k), row, col)

    def at_z(z):
        return (y, z * RING + x, col)

    to_far = (y, row, far)
    to_sib = (y, row, sib)
    flip = (zl, y * RING + col, x)
    off_diagonal = row != y * RING + col

    count = [0, 0]
    open_sends = []

    def copy(src, dst, device, recv=None):
        i = count[0]
        count[0] += 1
        if recv is None:
            recv = count[1]
            count[1] += 1
        return pltpu.make_async_remote_copy(
            src_ref=src, dst_ref=dst, send_sem=send_sem.at[i], recv_sem=recv_sem.at[recv],
            device_id=device, device_id_type=MESH)

    def push(src, dst, device, recv=None):
        c = copy(src, dst, device, recv)
        c.start()
        open_sends.append((always, c))
        return c

    loads = [pltpu.make_async_copy(x_hbm, xg.at[y, col], load_sem.at[0])]
    for b in range(OWN):
        loads.append(pltpu.make_async_copy(
            s_hbm.at[:, pl.ds(b * BLOCK, BLOCK)], sblk.at[b], load_sem.at[1 + b]))
    loads.append(pltpu.make_async_copy(w_hbm, wv, load_sem.at[1 + OWN]))
    for c in loads:
        c.start()

    kin[...] = jnp.zeros_like(kin)
    barrier = pltpu.get_barrier_semaphore()
    peers = [to_far, to_sib]
    for k in (1, 2, 3):
        peers += [to_x(k), to_y(k), at_z(wrap(zl + k))]
    for p in peers:
        pl.semaphore_signal(barrier, inc=1, device_id=p, device_id_type=MESH)

    @pl.when(off_diagonal)
    def _():
        pl.semaphore_signal(barrier, inc=1, device_id=flip, device_id_type=MESH)

    pl.semaphore_wait(barrier, len(peers) + off_diagonal.astype(jnp.int32))

    class Gather:
        def __init__(self, buf, own):
            self.buf = buf
            slot = buf.at[y, col]
            self.far = push(own, slot, to_far)
            self.sib = {(0, 0): push(own, slot, to_sib)}
            self.near = {(k, 0): push(own, slot, to_y(k)) for k in ORDER[1:]}

        def spread(self):
            self.far.wait_recv()
            piece = self.buf.at[y, far]
            self.sib[0, 1] = push(piece, piece, to_sib)
            for k in ORDER[1:]:
                self.near[k, 1] = push(piece, piece, to_y(k))

        def hand(self, k, w):
            self.near[k, w].wait_recv()
            piece = self.buf.at[wrap(y - k), far if w else col]
            self.sib[k, w] = push(piece, piece, to_sib)

        def ready(self, k, w):
            self.sib[k, w].wait_recv()

    loads[0].wait()
    gx = Gather(xg, xg.at[y, col])

    for b in range(OWN):
        loads[1 + b].wait()
    student = []
    for k in (1, 3, 2, 0):
        xt = wrap(x + k)
        for j in range(SLOTS):
            pick = jnp.int32(0)
            for zt in range(RING):
                p = kept[(zt * RING + xt) * SLOTS + j] - row * OWN
                pick = jnp.where((p >= 0) & (p < OWN), p, pick)
            if k == 0:
                sx[x * SLOTS + j] = sblk[pick]
            else:
                packx[(k - 1) * SLOTS + j] = sblk[pick]
        if k:
            student.append(push(packx.at[pl.ds((k - 1) * SLOTS, SLOTS)],
                                sx.at[pl.ds(x * SLOTS, SLOTS)], to_x(k)))

    def linked(src, dst):
        gap = dst - src
        return (gap == 1) | (gap == -1) | ((src == 2) & (dst == 0)) | ((src == 1) & (dst == 3))

    packs = []

    def send_packs():
        for c in student:
            c.wait_recv()
        for k in range(RING):
            zt = wrap(zl + k)
            for j in range(SLOTS):
                p = kept[(zt * RING + x) * SLOTS + j]
                block = sx[lax.rem(lax.div(p, OWN), RING) * SLOTS + j]
                if k == 0:
                    kin[zl * SLOTS + j] = block
                else:
                    packz[(k - 1) * SLOTS + j] = block
            if k:
                c = copy(packz.at[pl.ds((k - 1) * SLOTS, SLOTS)],
                         kin.at[pl.ds(zl * SLOTS, SLOTS)], at_z(zt))
                packs.append((k, c))
                goes = pl.when(linked(zl, zt))
                goes(c.start)
                open_sends.append((goes, c))

    def make_tile():
        for k, c in packs:
            pl.when(linked(wrap(zl - k), zl))(c.wait_recv)
        for j in range(SLOTS):
            p = kept[row * SLOTS + j]
            tile[:, j * BLOCK:(j + 1) * BLOCK] = kin[lax.div(p, RING * OWN) * SLOTS + j]
        kr[y, col] = tile[...]

    rsx, rsz, mid, agz, agx, fwd = {}, {}, {}, {}, {}, {}
    place = [(wrap(y - k), lax.rem(zh + w, 2)) for k, w in CHUNKS]

    def stage_a(i):
        k, w = CHUNKS[i]
        gx.ready(k, w)
        q, h = place[i]
        lhs = xg[q, pl.ds(2 * h, 2)].reshape(PAIR, FEAT)
        out = jnp.dot(lhs, wv[...], preferred_element_type=F32)
        part[i] = out.astype(BF16)
        mine[...] = out
        for n, k in enumerate((1, 3, 2)):
            rsx[i, n] = push(part.at[i, pl.ds(wrap(x + k) * SUB, SUB)], xin.at[i, n], to_x(k))
        total[i] = mine[pl.ds(x * SUB, SUB)]

    def stage_b(i):
        for n in range(3):
            rsx[i, n].wait_recv()
        total[i] = (total[i] + xin[i, 0].astype(F32)) + (xin[i, 1].astype(F32) + xin[i, 2].astype(F32))
        c = copy(total.at[i], zin.at[i], at_z(jnp.where(zl < 2, 1, 2)))
        pl.when(outer)(c.start)
        open_sends.append((pl.when(outer), c))
        rsz[i] = c

    def stage_c(i):
        c = copy(total.at[i, pl.ds(lax.rem(zl, 2) * HALF, HALF)], zhalf.at[i], at_z(3 - zl))
        mid[i] = c
        open_sends.append((pl.when(inner), c))

        @pl.when(inner)
        def _():
            rsz[i].wait_recv()
            total[i] = total[i] + zin[i]
            c.start()

    def stage_d(i):
        h = lax.rem(zl + 1, 2)
        rows = pl.ds(h * HALF, HALF)
        q, g = place[i]
        piece = tg.at[q, g, x, rows]
        base = count[1]
        count[1] += 2
        cs = [copy(piece, piece, at_z(wrap(zl + k)), base + h) for k in (1, 2, 3)]
        agz[i] = base
        for c in cs:
            open_sends.append((pl.when(inner), c))

        @pl.when(inner)
        def _():
            mid[i].wait_recv()
            tg[q, g, x, rows] = (total[i, rows] + zhalf[i]).astype(BF16)
            for c in cs:
                c.start()

    def stage_e(i):
        q, g = place[i]
        for h in (0, 1):
            piece = tg.at[q, g, x, pl.ds(h * HALF, HALF)]
            c = pltpu.make_async_remote_copy(
                src_ref=piece, dst_ref=piece, send_sem=send_sem.at[0],
                recv_sem=recv_sem.at[agz[i] + h], device_id=to_sib, device_id_type=MESH)
            pl.when(zl != h + 1)(c.wait_recv)
        piece = tg.at[q, g, x]
        for k in (1, 3):
            agx[i, k] = push(piece, piece, to_x(k))

    def stage_f(i):
        q, g = place[i]
        for k, lo in ((1, 0), (3, HALF)):
            agx[i, k].wait_recv()
            piece = tg.at[q, g, wrap(x - k), pl.ds(lo, HALF)]
            fwd[i, k] = push(piece, piece, to_x(k))

    def stage_g(i):
        for k in (1, 3):
            fwd[i, k].wait_recv()
        q, g = place[i]
        lhs = kr[q, pl.ds(2 * g, 2)].reshape(PAIR, KEPT)
        rhs = tg[q, g].reshape(PAIR, FEAT)
        out = lax.dot_general(lhs, rhs, (((0,), (0,)), ((), ())), preferred_element_type=F32)
        if i == 0:
            cross_ref[...] = out
        elif i < len(CHUNKS) - 1:
            cross_ref[...] += out
        else:
            cross_ref[...] = (cross_ref[...] + out) * INV

    loads[1 + OWN].wait()
    stage_a(0)
    send_packs()
    gx.hand(*CHUNKS[1])
    gx.hand(*CHUNKS[2])
    stage_a(1)
    stage_b(0)
    make_tile()
    gk = Gather(kr, tile)
    share = copy(tile, kc.at[col, y], flip)
    pl.when(off_diagonal)(share.start)
    open_sends.append((pl.when(off_diagonal), share))

    @pl.when(jnp.logical_not(off_diagonal))
    def _():
        kc[x, zl] = tile[...]

    stage_a(2)
    gx.spread()
    gx.hand(*CHUNKS[3])
    stage_b(1)
    stage_c(0)
    stage_a(3)
    stage_b(2)
    stage_c(1)
    stage_d(0)
    stage_a(4)
    gk.spread()
    gx.hand(*CHUNKS[5])
    stage_b(3)
    stage_c(2)
    stage_d(1)
    stage_e(0)
    stage_a(5)
    pl.when(off_diagonal)(share.wait_recv)
    own_share = kc.at[x, zl]
    colz = [push(own_share, own_share, at_z(wrap(zl + k))) for k in (1, 2, 3)]
    gx.hand(*CHUNKS[6])
    stage_b(4)
    stage_c(3)
    stage_d(2)
    stage_e(1)
    stage_f(0)
    stage_a(6)
    gx.hand(*CHUNKS[7])
    for k in ORDER[1:]:
        gk.hand(k, 0)
    stage_b(5)
    stage_c(4)
    stage_d(3)
    stage_e(2)
    stage_f(1)
    stage_a(7)
    for k in ORDER[1:]:
        gk.hand(k, 1)
    stage_b(6)
    stage_c(5)
    stage_d(4)
    stage_e(3)
    stage_f(2)
    for c in colz:
        c.wait_recv()
    colx = {k: push(kc.at[x], kc.at[x], to_x(k)) for k in (1, 3)}
    for k, w in CHUNKS:
        gk.ready(k, w)
    stage_g(0)
    stage_b(7)
    stage_c(6)
    stage_d(5)
    stage_e(4)
    stage_f(3)
    stage_g(1)
    stage_c(7)
    stage_d(6)
    stage_e(5)
    stage_f(4)
    stage_g(2)
    colf = {}
    for k, lo in ((1, 0), (3, 2)):
        colx[k].wait_recv()
        piece = kc.at[wrap(x - k), pl.ds(lo, 2)]
        colf[k] = push(piece, piece, to_x(k))
    stage_d(7)
    stage_e(6)
    stage_f(5)
    stage_g(3)
    stage_e(7)
    stage_f(6)
    stage_g(4)
    for k in (1, 3):
        colf[k].wait_recv()

    def gram_body(j, carry):
        lhs = kr[:, j].reshape(RING * TOK, KEPT)
        rhs = kc[j].reshape(RING * TOK, KEPT)
        gram_ref[...] += lax.dot_general(lhs, rhs, (((0,), (0,)), ((), ())), preferred_element_type=F32)
        return carry

    gram_ref[...] = jnp.zeros_like(gram_ref)
    lax.fori_loop(0, RING, gram_body, 0)
    gram_ref[...] = gram_ref[...] * INV
    stage_f(7)
    stage_g(5)
    stage_g(6)
    stage_g(7)

    for when, c in open_sends:
        when(c.wait_send)


def local(teacher_in, weight, student_in, kept_blocks):
    vmem = pl.BlockSpec(memory_space=pltpu.VMEM)
    hbm = pl.BlockSpec(memory_space=pltpu.HBM)
    n = len(CHUNKS)
    return pl.pallas_call(
        kernel,
        out_shape=(jax.ShapeDtypeStruct((KEPT, KEPT), F32),
                   jax.ShapeDtypeStruct((KEPT, FEAT), F32)),
        in_specs=[pl.BlockSpec(memory_space=pltpu.SMEM), hbm, hbm, hbm],
        out_specs=(vmem, vmem),
        scratch_shapes=[
            pltpu.VMEM((RING, RING, TOK, FEAT), BF16),
            pltpu.VMEM((FEAT, FEAT), BF16),
            pltpu.VMEM((OWN, TOK, BLOCK), BF16),
            pltpu.VMEM((n, PAIR, FEAT), BF16),
            pltpu.VMEM((PAIR, FEAT), F32),
            pltpu.VMEM((n, 3, SUB, FEAT), BF16),
            pltpu.VMEM((n, SUB, FEAT), F32),
            pltpu.VMEM((n, SUB, FEAT), F32),
            pltpu.VMEM((n, HALF, FEAT), F32),
            pltpu.VMEM((RING, 2, RING, SUB, FEAT), BF16),
            pltpu.VMEM((3 * SLOTS, TOK, BLOCK), BF16),
            pltpu.VMEM((RING * SLOTS, TOK, BLOCK), BF16),
            pltpu.VMEM((3 * SLOTS, TOK, BLOCK), BF16),
            pltpu.VMEM((RING * SLOTS, TOK, BLOCK), BF16),
            pltpu.VMEM((TOK, KEPT), BF16),
            pltpu.VMEM((RING, RING, TOK, KEPT), BF16),
            pltpu.VMEM((RING, RING, TOK, KEPT), BF16),
            pltpu.SemaphoreType.DMA((2 + OWN,)),
            pltpu.SemaphoreType.DMA((COPIES,)),
            pltpu.SemaphoreType.DMA((COPIES,)),
        ],
        compiler_params=pltpu.CompilerParams(
            collective_id=0, has_side_effects=True, vmem_limit_bytes=48 << 20),
        name="gram_cross",
    )(kept_blocks, teacher_in, weight, student_in)


def solution(mesh):
    return jax.shard_map(
        local,
        mesh=mesh,
        in_specs=(
            P(("grp", "col"), "row"),
            P("row", ("grp", "col")),
            P(("grp", "col"), "row"),
            P(),
        ),
        out_specs=(P("row", ("grp", "col")), P("row", ("grp", "col"))),
        check_vma=False,
    )
```

```python
import jax
import jax.numpy as jnp
from jax import lax
from jax.experimental import pallas as pl
from jax.experimental.pallas import tpu as pltpu
from jax.sharding import PartitionSpec as P

MESH = pl.DeviceIdType.MESH
F32 = jnp.float32
BF16 = jnp.bfloat16
RING = 4
TOK = 128
PAIR = 2 * TOK
SUB = PAIR // RING
HALF = SUB // 2
FEAT = 768
KEPT = 384
BLOCK = 128
OWN = FEAT // BLOCK
SLOTS = KEPT // BLOCK
ORDER = (0, 1, 3, 2)
CHUNKS = tuple((k, w) for w in (0, 1) for k in ORDER)
INV = 1.0 / 2048
COPIES = 180
VMEM = 65273856


def wrap(v):
    return lax.rem(v + RING, RING)


def always(body):
    body()


def kernel(kept, x_hbm, w_hbm, s_hbm, gram_ref, cross_ref,
           xg, wv, sblk, part, mine, xin, total, zin, zhalf, tg,
           packx, sx, packz, kin, tile, kr, kc,
           load_sem, send_sem, recv_sem):
    y, row, col = lax.axis_index("grp"), lax.axis_index("row"), lax.axis_index("col")
    zl, x = lax.div(row, RING), lax.rem(row, RING)
    zh, core = lax.div(col, 2), lax.rem(col, 2)
    sib = col + 1 - 2 * core
    far = wrap(col + 2)
    inner = (zl == 1) | (zl == 2)
    outer = jnp.logical_not(inner)

    def to_x(k):
        return (y, zl * RING + wrap(x + k), col)

    def to_y(k):
        return (wrap(y + k), row, col)

    def at_z(z):
        return (y, z * RING + x, col)

    to_far = (y, row, far)
    to_sib = (y, row, sib)
    flip = (zl, y * RING + col, x)
    off_diagonal = row != y * RING + col

    count = [0, 0]
    open_sends = []
    owed = {}
    done = []

    def copy(src, dst, device, recv=None):
        i = count[0]
        count[0] += 1
        if recv is None:
            recv = count[1]
            count[1] += 1
        return pltpu.make_async_remote_copy(
            src_ref=src, dst_ref=dst, send_sem=send_sem.at[i], recv_sem=recv_sem.at[recv],
            device_id=device, device_id_type=MESH)

    def push(src, dst, device, recv=None):
        c = copy(src, dst, device, recv)
        c.start()
        open_sends.append((always, c))
        owed[id(c)] = (always, c)
        return c

    def got(c):
        when, c = owed.pop(id(c))
        when(c.wait_recv)

    loads = [pltpu.make_async_copy(x_hbm, xg.at[y, col], load_sem.at[0])]
    for b in range(OWN):
        loads.append(pltpu.make_async_copy(
            s_hbm.at[:, pl.ds(b * BLOCK, BLOCK)], sblk.at[b], load_sem.at[1 + b]))
    loads.append(pltpu.make_async_copy(w_hbm, wv, load_sem.at[1 + OWN]))
    for c in loads:
        c.start()

    kin[...] = jnp.zeros_like(kin)
    barrier = pltpu.get_barrier_semaphore()
    peers = [to_far, to_sib]
    for k in (1, 2, 3):
        peers += [to_x(k), to_y(k), at_z(wrap(zl + k))]
    for p in peers:
        pl.semaphore_signal(barrier, inc=1, device_id=p, device_id_type=MESH)

    @pl.when(off_diagonal)
    def _():
        pl.semaphore_signal(barrier, inc=1, device_id=flip, device_id_type=MESH)

    pl.semaphore_wait(barrier, len(peers) + off_diagonal.astype(jnp.int32))

    class Gather:
        def __init__(self, buf, own):
            self.buf = buf
            slot = buf.at[y, col]
            self.far = push(own, slot, to_far)
            self.sib = {(0, 0): push(own, slot, to_sib)}
            self.near = {(k, 0): push(own, slot, to_y(k)) for k in ORDER[1:]}

        def spread(self):
            got(self.far)
            piece = self.buf.at[y, far]
            self.sib[0, 1] = push(piece, piece, to_sib)
            for k in ORDER[1:]:
                self.near[k, 1] = push(piece, piece, to_y(k))

        def hand(self, k, w):
            got(self.near[k, w])
            piece = self.buf.at[wrap(y - k), far if w else col]
            self.sib[k, w] = push(piece, piece, to_sib)

        def ready(self, k, w):
            got(self.sib[k, w])

    loads[0].wait()
    gx = Gather(xg, xg.at[y, col])

    for b in range(OWN):
        loads[1 + b].wait()
    student = []
    for k in (1, 3, 2, 0):
        xt = wrap(x + k)
        for j in range(SLOTS):
            pick = jnp.int32(0)
            for zt in range(RING):
                p = kept[(zt * RING + xt) * SLOTS + j] - row * OWN
                pick = jnp.where((p >= 0) & (p < OWN), p, pick)
            if k == 0:
                sx[x * SLOTS + j] = sblk[pick]
            else:
                packx[(k - 1) * SLOTS + j] = sblk[pick]
        if k:
            student.append(push(packx.at[pl.ds((k - 1) * SLOTS, SLOTS)],
                                sx.at[pl.ds(x * SLOTS, SLOTS)], to_x(k)))

    def linked(src, dst):
        gap = dst - src
        return (gap == 1) | (gap == -1) | ((src == 2) & (dst == 0)) | ((src == 1) & (dst == 3))

    packs = []

    def send_packs():
        for c in student:
            got(c)
        for k in range(RING):
            zt = wrap(zl + k)
            for j in range(SLOTS):
                p = kept[(zt * RING + x) * SLOTS + j]
                block = sx[lax.rem(lax.div(p, OWN), RING) * SLOTS + j]
                if k == 0:
                    kin[zl * SLOTS + j] = block
                else:
                    packz[(k - 1) * SLOTS + j] = block
            if k:
                c = copy(packz.at[pl.ds((k - 1) * SLOTS, SLOTS)],
                         kin.at[pl.ds(zl * SLOTS, SLOTS)], at_z(zt))
                packs.append((k, c))
                goes = pl.when(linked(zl, zt))
                goes(c.start)
                open_sends.append((goes, c))
                owed[id(c)] = (pl.when(linked(wrap(zl - k), zl)), c)

    def make_tile():
        for k, c in packs:
            got(c)
        for j in range(SLOTS):
            p = kept[row * SLOTS + j]
            tile[:, j * BLOCK:(j + 1) * BLOCK] = kin[lax.div(p, RING * OWN) * SLOTS + j]
        kr[y, col] = tile[...]

    rsx, rsz, mid, agz, agx, fwd = {}, {}, {}, {}, {}, {}
    place = [(wrap(y - k), lax.rem(zh + w, 2)) for k, w in CHUNKS]

    def stage_a(i):
        k, w = CHUNKS[i]
        gx.ready(k, w)
        q, h = place[i]
        lhs = xg[q, pl.ds(2 * h, 2)].reshape(PAIR, FEAT)
        out = jnp.dot(lhs, wv[...], preferred_element_type=F32)
        part[i] = out.astype(BF16)
        mine[...] = out
        for n, k in enumerate((1, 3, 2)):
            rsx[i, n] = push(part.at[i, pl.ds(wrap(x + k) * SUB, SUB)], xin.at[i, n], to_x(k))
        total[i] = mine[pl.ds(x * SUB, SUB)]

    def stage_b(i):
        for n in range(3):
            got(rsx[i, n])
        total[i] = (total[i] + xin[i, 0].astype(F32)) + (xin[i, 1].astype(F32) + xin[i, 2].astype(F32))
        c = copy(total.at[i], zin.at[i], at_z(jnp.where(zl < 2, 1, 2)))
        pl.when(outer)(c.start)
        open_sends.append((pl.when(outer), c))
        owed[id(c)] = (pl.when(inner), c)
        rsz[i] = c

    def stage_c(i):
        c = copy(total.at[i, pl.ds(lax.rem(zl, 2) * HALF, HALF)], zhalf.at[i], at_z(3 - zl))
        mid[i] = c
        owed[id(c)] = (pl.when(inner), c)
        open_sends.append((pl.when(inner), c))

        got(rsz[i])

        @pl.when(inner)
        def _():
            total[i] = total[i] + zin[i]
            c.start()

    def stage_d(i):
        h = lax.rem(zl + 1, 2)
        rows = pl.ds(h * HALF, HALF)
        q, g = place[i]
        piece = tg.at[q, g, x, rows]
        base = count[1]
        count[1] += 2
        cs = [copy(piece, piece, at_z(wrap(zl + k)), base + h) for k in (1, 2, 3)]
        agz[i] = []
        for n in (0, 1):
            c = pltpu.make_async_remote_copy(
                src_ref=tg.at[q, g, x, pl.ds(n * HALF, HALF)],
                dst_ref=tg.at[q, g, x, pl.ds(n * HALF, HALF)], send_sem=send_sem.at[0],
                recv_sem=recv_sem.at[base + n], device_id=to_sib, device_id_type=MESH)
            owed[id(c)] = (pl.when(zl != n + 1), c)
            agz[i].append(c)
        for c in cs:
            open_sends.append((pl.when(inner), c))

        got(mid[i])

        @pl.when(inner)
        def _():
            tg[q, g, x, rows] = (total[i, rows] + zhalf[i]).astype(BF16)
            for c in cs:
                c.start()

    def stage_e(i):
        q, g = place[i]
        for c in agz[i]:
            got(c)
        piece = tg.at[q, g, x]
        for k in (1, 3):
            agx[i, k] = push(piece, piece, to_x(k))

    def stage_f(i):
        q, g = place[i]
        for k, lo in ((1, 0), (3, HALF)):
            got(agx[i, k])
            piece = tg.at[q, g, wrap(x - k), pl.ds(lo, HALF)]
            fwd[i, k] = push(piece, piece, to_x(k))

    def stage_g(i):
        for k in (1, 3):
            got(fwd[i, k])
        q, g = place[i]
        lhs = kr[q, pl.ds(2 * g, 2)].reshape(PAIR, KEPT)
        rhs = tg[q, g].reshape(PAIR, FEAT)
        out = lax.dot_general(lhs, rhs, (((0,), (0,)), ((), ())), preferred_element_type=F32)
        done.append(i)
        if len(done) == 1:
            cross_ref[...] = out
        elif len(done) < len(CHUNKS):
            cross_ref[...] += out
        else:
            cross_ref[...] = (cross_ref[...] + out) * INV

    def tile_out():
        make_tile()
        gather["k"] = Gather(kr, tile)
        c = copy(tile, kc.at[col, y], flip)
        pl.when(off_diagonal)(c.start)
        open_sends.append((pl.when(off_diagonal), c))
        owed[id(c)] = (pl.when(off_diagonal), c)
        share.append(c)

        @pl.when(jnp.logical_not(off_diagonal))
        def _():
            kc[x, zl] = tile[...]

    def hand(which, i):
        gather[which].hand(*CHUNKS[i])

    def spread(which):
        gather[which].spread()

    def share_z():
        got(share[0])
        piece = kc.at[x, zl]
        colz.extend(push(piece, piece, at_z(wrap(zl + k))) for k in (1, 2, 3))

    def share_x():
        for c in colz:
            got(c)
        for k in (1, 3):
            colx[k] = push(kc.at[x], kc.at[x], to_x(k))

    def share_fwd():
        for k, lo in ((1, 0), (3, 2)):
            got(colx[k])
            piece = kc.at[wrap(x - k), pl.ds(lo, 2)]
            colf[k] = push(piece, piece, to_x(k))

    def k_ready():
        for k, w in CHUNKS:
            gather["k"].ready(k, w)

    def gram():
        for k in (1, 3):
            got(colf[k])

        def gram_body(j, carry):
            lhs = kr[:, j].reshape(RING * TOK, KEPT)
            rhs = kc[j].reshape(RING * TOK, KEPT)
            gram_ref[...] += lax.dot_general(lhs, rhs, (((0,), (0,)), ((), ())), preferred_element_type=F32)
            return carry

        gram_ref[...] = jnp.zeros_like(gram_ref)
        lax.fori_loop(0, RING, gram_body, 0)
        gram_ref[...] = gram_ref[...] * INV

    gather, share, colz, colx, colf = {"x": gx}, [], [], {}, {}
    A, B, C, D, E, F, G = stage_a, stage_b, stage_c, stage_d, stage_e, stage_f, stage_g
    steps = (
        (loads[1 + OWN].wait,), (A, 0), (hand, "x", 2), (send_packs,), (A, 2), (spread, "x"), (B, 0),
        (A, 4), (hand, "x", 3), (tile_out,), (A, 3), (hand, "x", 5), (hand, "x", 1), (C, 0), (A, 5),
        (B, 2), (hand, "x", 7), (B, 3), (D, 0), (A, 1), (hand, "x", 6), (B, 4), (C, 2), (hand, "k", 3),
        (A, 6), (C, 3), (D, 2), (A, 7), (hand, "k", 1), (B, 5), (spread, "k"), (D, 3), (hand, "k", 6),
        (share_z,), (E, 0), (E, 2), (B, 7), (hand, "k", 2), (C, 5), (B, 1), (C, 4), (B, 6), (E, 3),
        (F, 0), (F, 2), (share_x,), (D, 5), (D, 4), (C, 1), (E, 5), (hand, "k", 7), (C, 7),
        (hand, "k", 5), (E, 4), (k_ready,), (C, 6), (D, 1), (share_fwd,), (G, 2), (F, 5), (D, 6),
        (D, 7), (E, 1), (E, 6), (G, 5), (E, 7), (F, 4), (G, 0), (F, 6), (F, 1), (gram,), (F, 7), (F, 3),
        (G, 4), (G, 1), (G, 6), (G, 7), (G, 3),
    )
    for step, *args in steps:
        step(*args)

    for when, c in tuple(owed.values()):
        when(c.wait_recv)
    for when, c in open_sends:
        when(c.wait_send)


def local(teacher_in, weight, student_in, kept_blocks):
    vmem = pl.BlockSpec(memory_space=pltpu.VMEM)
    hbm = pl.BlockSpec(memory_space=pltpu.HBM)
    n = len(CHUNKS)
    return pl.pallas_call(
        kernel,
        out_shape=(jax.ShapeDtypeStruct((KEPT, KEPT), F32),
                   jax.ShapeDtypeStruct((KEPT, FEAT), F32)),
        in_specs=[pl.BlockSpec(memory_space=pltpu.SMEM), hbm, hbm, hbm],
        out_specs=(vmem, vmem),
        scratch_shapes=[
            pltpu.VMEM((RING, RING, TOK, FEAT), BF16),
            pltpu.VMEM((FEAT, FEAT), BF16),
            pltpu.VMEM((OWN, TOK, BLOCK), BF16),
            pltpu.VMEM((n, PAIR, FEAT), BF16),
            pltpu.VMEM((PAIR, FEAT), F32),
            pltpu.VMEM((n, 3, SUB, FEAT), BF16),
            pltpu.VMEM((n, SUB, FEAT), F32),
            pltpu.VMEM((n, SUB, FEAT), F32),
            pltpu.VMEM((n, HALF, FEAT), F32),
            pltpu.VMEM((RING, 2, RING, SUB, FEAT), BF16),
            pltpu.VMEM((3 * SLOTS, TOK, BLOCK), BF16),
            pltpu.VMEM((RING * SLOTS, TOK, BLOCK), BF16),
            pltpu.VMEM((3 * SLOTS, TOK, BLOCK), BF16),
            pltpu.VMEM((RING * SLOTS, TOK, BLOCK), BF16),
            pltpu.VMEM((TOK, KEPT), BF16),
            pltpu.VMEM((RING, RING, TOK, KEPT), BF16),
            pltpu.VMEM((RING, RING, TOK, KEPT), BF16),
            pltpu.SemaphoreType.DMA((2 + OWN,)),
            pltpu.SemaphoreType.DMA((COPIES,)),
            pltpu.SemaphoreType.DMA((COPIES,)),
        ],
        compiler_params=pltpu.CompilerParams(
            collective_id=0, has_side_effects=True, vmem_limit_bytes=VMEM),
        name="gram_cross",
    )(kept_blocks, teacher_in, weight, student_in)


def solution(mesh):
    return jax.shard_map(
        local,
        mesh=mesh,
        in_specs=(
            P(("grp", "col"), "row"),
            P("row", ("grp", "col")),
            P(("grp", "col"), "row"),
            P(),
        ),
        out_specs=(P("row", ("grp", "col")), P("row", ("grp", "col"))),
        check_vma=False,
    )
```

```python
import jax
import jax.numpy as jnp
from jax import lax
from jax.experimental import pallas as pl
from jax.experimental.pallas import tpu as pltpu
from jax.sharding import PartitionSpec as P

MESH = pl.DeviceIdType.MESH
F32 = jnp.float32
BF16 = jnp.bfloat16
RING = 4
TOK = 128
PAIR = 2 * TOK
SUB = PAIR // RING
HALF = SUB // 2
FEAT = 768
KEPT = 384
BLOCK = 128
OWN = FEAT // BLOCK
SLOTS = KEPT // BLOCK
ORDER = (0, 1, 3, 2)
CHUNKS = tuple((k, w) for w in (0, 1) for k in ORDER)
INV = 1.0 / 2048
COPIES = 240
RELAYED = (0, 0, 0, 0, 1, 1, 1, 1)
VMEM = 65273856


def wrap(v):
    return lax.rem(v + RING, RING)


def always(body):
    body()


def kernel(kept, x_hbm, w_hbm, s_hbm, gram_ref, cross_ref,
           xg, wv, sblk, part, mine, hopin, both, xin, total, zin, zhalf, tg,
           packx, sx, packz, kin, tile, kr, kc,
           load_sem, send_sem, recv_sem):
    y, row, col = lax.axis_index("grp"), lax.axis_index("row"), lax.axis_index("col")
    zl, x = lax.div(row, RING), lax.rem(row, RING)
    zh, core = lax.div(col, 2), lax.rem(col, 2)
    sib = col + 1 - 2 * core
    far = wrap(col + 2)
    inner = (zl == 1) | (zl == 2)
    outer = jnp.logical_not(inner)

    def to_x(k):
        return (y, zl * RING + wrap(x + k), col)

    def to_y(k):
        return (wrap(y + k), row, col)

    def at_z(z):
        return (y, z * RING + x, col)

    to_far = (y, row, far)
    to_sib = (y, row, sib)
    flip = (zl, y * RING + col, x)
    off_diagonal = row != y * RING + col

    count = [0, 0]
    open_sends = []
    owed = {}
    done = []

    def copy(src, dst, device, recv=None):
        i = count[0]
        count[0] += 1
        if recv is None:
            recv = count[1]
            count[1] += 1
        return pltpu.make_async_remote_copy(
            src_ref=src, dst_ref=dst, send_sem=send_sem.at[i], recv_sem=recv_sem.at[recv],
            device_id=device, device_id_type=MESH)

    def push(src, dst, device, recv=None):
        c = copy(src, dst, device, recv)
        c.start()
        open_sends.append((always, c))
        owed[id(c)] = (always, c)
        return c

    def got(c):
        when, c = owed.pop(id(c))
        when(c.wait_recv)

    loads = [pltpu.make_async_copy(x_hbm, xg.at[y, col], load_sem.at[0])]
    for b in range(OWN):
        loads.append(pltpu.make_async_copy(
            s_hbm.at[:, pl.ds(b * BLOCK, BLOCK)], sblk.at[b], load_sem.at[1 + b]))
    loads.append(pltpu.make_async_copy(w_hbm, wv, load_sem.at[1 + OWN]))
    for c in loads:
        c.start()

    kin[...] = jnp.zeros_like(kin)
    barrier = pltpu.get_barrier_semaphore()
    peers = [to_far, to_sib]
    for k in (1, 2, 3):
        peers += [to_x(k), to_y(k), at_z(wrap(zl + k))]
    for p in peers:
        pl.semaphore_signal(barrier, inc=1, device_id=p, device_id_type=MESH)

    @pl.when(off_diagonal)
    def _():
        pl.semaphore_signal(barrier, inc=1, device_id=flip, device_id_type=MESH)

    pl.semaphore_wait(barrier, len(peers) + off_diagonal.astype(jnp.int32))

    class Gather:
        def __init__(self, buf, own):
            self.buf = buf
            slot = buf.at[y, col]
            self.far = push(own, slot, to_far)
            self.sib = {(0, 0): push(own, slot, to_sib)}
            self.near = {(k, 0): push(own, slot, to_y(k)) for k in ORDER[1:]}

        def spread(self):
            got(self.far)
            piece = self.buf.at[y, far]
            self.sib[0, 1] = push(piece, piece, to_sib)
            for k in ORDER[1:]:
                self.near[k, 1] = push(piece, piece, to_y(k))

        def hand(self, k, w):
            got(self.near[k, w])
            piece = self.buf.at[wrap(y - k), far if w else col]
            self.sib[k, w] = push(piece, piece, to_sib)

        def ready(self, k, w):
            got(self.sib[k, w])

    loads[0].wait()
    gx = Gather(xg, xg.at[y, col])

    for b in range(OWN):
        loads[1 + b].wait()
    student = []
    for k in (1, 3, 2, 0):
        xt = wrap(x + k)
        for j in range(SLOTS):
            pick = jnp.int32(0)
            for zt in range(RING):
                p = kept[(zt * RING + xt) * SLOTS + j] - row * OWN
                pick = jnp.where((p >= 0) & (p < OWN), p, pick)
            if k == 0:
                sx[x * SLOTS + j] = sblk[pick]
            else:
                packx[(k - 1) * SLOTS + j] = sblk[pick]
        if k:
            student.append(push(packx.at[pl.ds((k - 1) * SLOTS, SLOTS)],
                                sx.at[pl.ds(x * SLOTS, SLOTS)], to_x(k)))

    def linked(src, dst):
        gap = dst - src
        return (gap == 1) | (gap == -1) | ((src == 2) & (dst == 0)) | ((src == 1) & (dst == 3))

    packs = []

    def send_packs():
        for c in student:
            got(c)
        for k in range(RING):
            zt = wrap(zl + k)
            for j in range(SLOTS):
                p = kept[(zt * RING + x) * SLOTS + j]
                block = sx[lax.rem(lax.div(p, OWN), RING) * SLOTS + j]
                if k == 0:
                    kin[zl * SLOTS + j] = block
                else:
                    packz[(k - 1) * SLOTS + j] = block
            if k:
                c = copy(packz.at[pl.ds((k - 1) * SLOTS, SLOTS)],
                         kin.at[pl.ds(zl * SLOTS, SLOTS)], at_z(zt))
                packs.append((k, c))
                goes = pl.when(linked(zl, zt))
                goes(c.start)
                open_sends.append((goes, c))
                owed[id(c)] = (pl.when(linked(wrap(zl - k), zl)), c)

    def make_tile():
        for k, c in packs:
            got(c)
        for j in range(SLOTS):
            p = kept[row * SLOTS + j]
            tile[:, j * BLOCK:(j + 1) * BLOCK] = kin[lax.div(p, RING * OWN) * SLOTS + j]
        kr[y, col] = tile[...]

    hop, rsx, rsz, mid, agz, agx, fwd = {}, {}, {}, {}, {}, {}, {}
    place = [(wrap(y - k), lax.rem(zh + w, 2)) for k, w in CHUNKS]

    def stage_a(i):
        k, w = CHUNKS[i]
        gx.ready(k, w)
        q, h = place[i]
        lhs = xg[q, pl.ds(2 * h, 2)].reshape(PAIR, FEAT)
        out = jnp.dot(lhs, wv[...], preferred_element_type=F32)
        part[i] = out.astype(BF16)
        mine[i] = out
        if not RELAYED[i]:
            for n, k in enumerate((1, 3, 2)):
                rsx[i, n, 0] = push(part.at[i, pl.ds(wrap(x + k) * SUB, SUB)], xin.at[i, n], to_x(k))
            return
        for n, k in enumerate((1, 3)):
            hop[i, n] = push(part.at[i, pl.ds(wrap(x + 2) * SUB + n * HALF, HALF)], hopin.at[i, n], to_x(k))
        for n, k in enumerate((1, 3)):
            lo = (1 - n) * HALF
            rsx[i, n, 0] = push(part.at[i, pl.ds(wrap(x + k) * SUB + lo, HALF)],
                                xin.at[i, n, pl.ds(lo, HALF)], to_x(k))

    def stage_h(i):
        for n, k in enumerate((1, 3)):
            got(hop[i, n])
            rows = pl.ds(wrap(x + k) * SUB + n * HALF, HALF)
            both[i, n] = (mine[i, rows] + hopin[i, n].astype(F32)).astype(BF16)
            rsx[i, n, 1] = push(both.at[i, n], xin.at[i, n, pl.ds(n * HALF, HALF)], to_x(k))

    def stage_b(i):
        own = mine[i, pl.ds(x * SUB, SUB)]
        for n in range(2 if RELAYED[i] else 3):
            for m in range(2 if RELAYED[i] else 1):
                got(rsx[i, n, m])
        if not RELAYED[i]:
            own = own + xin[i, 2].astype(F32)
        total[i] = own + (xin[i, 0].astype(F32) + xin[i, 1].astype(F32))
        c = copy(total.at[i], zin.at[i], at_z(jnp.where(zl < 2, 1, 2)))
        pl.when(outer)(c.start)
        open_sends.append((pl.when(outer), c))
        owed[id(c)] = (pl.when(inner), c)
        rsz[i] = c

    def stage_c(i):
        c = copy(total.at[i, pl.ds(lax.rem(zl, 2) * HALF, HALF)], zhalf.at[i], at_z(3 - zl))
        mid[i] = c
        owed[id(c)] = (pl.when(inner), c)
        open_sends.append((pl.when(inner), c))

        got(rsz[i])

        @pl.when(inner)
        def _():
            total[i] = total[i] + zin[i]
            c.start()

    def stage_d(i):
        h = lax.rem(zl + 1, 2)
        rows = pl.ds(h * HALF, HALF)
        q, g = place[i]
        piece = tg.at[q, g, x, rows]
        base = count[1]
        count[1] += 2
        cs = [copy(piece, piece, at_z(wrap(zl + k)), base + h) for k in (1, 2, 3)]
        agz[i] = []
        for n in (0, 1):
            c = pltpu.make_async_remote_copy(
                src_ref=tg.at[q, g, x, pl.ds(n * HALF, HALF)],
                dst_ref=tg.at[q, g, x, pl.ds(n * HALF, HALF)], send_sem=send_sem.at[0],
                recv_sem=recv_sem.at[base + n], device_id=to_sib, device_id_type=MESH)
            owed[id(c)] = (pl.when(zl != n + 1), c)
            agz[i].append(c)
        for c in cs:
            open_sends.append((pl.when(inner), c))

        got(mid[i])

        @pl.when(inner)
        def _():
            tg[q, g, x, rows] = (total[i, rows] + zhalf[i]).astype(BF16)
            for c in cs:
                c.start()

    def stage_e(i):
        q, g = place[i]
        for c in agz[i]:
            got(c)
        piece = tg.at[q, g, x]
        for k in (1, 3):
            agx[i, k] = push(piece, piece, to_x(k))

    def stage_f(i):
        q, g = place[i]
        for k, lo in ((1, 0), (3, HALF)):
            got(agx[i, k])
            piece = tg.at[q, g, wrap(x - k), pl.ds(lo, HALF)]
            fwd[i, k] = push(piece, piece, to_x(k))

    def stage_g(i):
        for k in (1, 3):
            got(fwd[i, k])
        q, g = place[i]
        lhs = kr[q, pl.ds(2 * g, 2)].reshape(PAIR, KEPT)
        rhs = tg[q, g].reshape(PAIR, FEAT)
        out = lax.dot_general(lhs, rhs, (((0,), (0,)), ((), ())), preferred_element_type=F32)
        done.append(i)
        if len(done) == 1:
            cross_ref[...] = out
        elif len(done) < len(CHUNKS):
            cross_ref[...] += out
        else:
            cross_ref[...] = (cross_ref[...] + out) * INV

    def tile_out():
        make_tile()
        gather["k"] = Gather(kr, tile)
        c = copy(tile, kc.at[col, y], flip)
        pl.when(off_diagonal)(c.start)
        open_sends.append((pl.when(off_diagonal), c))
        owed[id(c)] = (pl.when(off_diagonal), c)
        share.append(c)

        @pl.when(jnp.logical_not(off_diagonal))
        def _():
            kc[x, zl] = tile[...]

    def hand(which, i):
        gather[which].hand(*CHUNKS[i])

    def spread(which):
        gather[which].spread()

    def share_here():
        if share:
            got(share.pop())
        return kc.at[x, zl]

    def share_z(k):
        piece = share_here()
        colz[k] = push(piece, piece, at_z(wrap(zl + k)))

    def share_x(k):
        if k:
            got(colz[k])
            piece = kc.at[x, wrap(zl - k)]
        else:
            piece = share_here()
        for d in (1, 3):
            colx[k, d] = push(piece, piece, to_x(d))

    def share_fwd(h):
        for k, d in ((2 * h, 1), (2 * h + 1, 3)):
            for e in (1, 3):
                got(colx[k, e])
            piece = kc.at[wrap(x - d), wrap(zl - k)]
            colf.append(push(piece, piece, to_x(d)))

    def k_ready():
        for k, w in CHUNKS:
            gather["k"].ready(k, w)

    def gram():
        for c in colf:
            got(c)

        def gram_body(j, carry):
            lhs = kr[:, j].reshape(RING * TOK, KEPT)
            rhs = kc[j].reshape(RING * TOK, KEPT)
            gram_ref[...] += lax.dot_general(lhs, rhs, (((0,), (0,)), ((), ())), preferred_element_type=F32)
            return carry

        gram_ref[...] = jnp.zeros_like(gram_ref)
        lax.fori_loop(0, RING, gram_body, 0)
        gram_ref[...] = gram_ref[...] * INV

    gather, share, colz, colx, colf = {"x": gx}, [], {}, {}, []
    A, H, B, C, D, E, F, G = stage_a, stage_h, stage_b, stage_c, stage_d, stage_e, stage_f, stage_g
    steps = (
        (loads[1 + OWN].wait,), (A, 0), (hand, "x", 1), (hand, "x", 2), (send_packs,), (A, 1),
        (spread, "x"), (B, 0), (A, 2), (tile_out,), (hand, "x", 5), (hand, "x", 6), (B, 1), (A, 5),
        (C, 0), (A, 4), (hand, "x", 7), (H, 5), (B, 2), (A, 7), (D, 0), (spread, "k"), (hand, "x", 3),
        (hand, "k", 3), (H, 4), (hand, "k", 1), (B, 5), (C, 1), (H, 7), (A, 6), (A, 3), (hand, "k", 6),
        (B, 4), (C, 2), (E, 0), (D, 1), (hand, "k", 7), (C, 5), (D, 2), (H, 6), (B, 7), (hand, "k", 5),
        (E, 1), (share_z, 1), (C, 4), (share_x, 0), (F, 0), (share_z, 3), (share_z, 2), (B, 3), (F, 1),
        (E, 2), (hand, "k", 2), (share_x, 1), (C, 7), (D, 4), (D, 5), (share_x, 3), (F, 2),
        (share_fwd, 0), (B, 6), (share_x, 2), (D, 7), (E, 4), (C, 3), (E, 5), (C, 6), (k_ready,),
        (share_fwd, 1), (E, 7), (D, 3), (F, 5), (D, 6), (F, 4), (E, 3), (G, 2), (E, 6), (G, 0), (G, 1),
        (G, 5), (F, 3), (G, 4), (F, 7), (F, 6), (gram,), (G, 3), (G, 7), (G, 6),
    )
    for step, *args in steps:
        step(*args)

    for when, c in tuple(owed.values()):
        when(c.wait_recv)
    for when, c in open_sends:
        when(c.wait_send)


def local(teacher_in, weight, student_in, kept_blocks):
    vmem = pl.BlockSpec(memory_space=pltpu.VMEM)
    hbm = pl.BlockSpec(memory_space=pltpu.HBM)
    n = len(CHUNKS)
    return pl.pallas_call(
        kernel,
        out_shape=(jax.ShapeDtypeStruct((KEPT, KEPT), F32),
                   jax.ShapeDtypeStruct((KEPT, FEAT), F32)),
        in_specs=[pl.BlockSpec(memory_space=pltpu.SMEM), hbm, hbm, hbm],
        out_specs=(vmem, vmem),
        scratch_shapes=[
            pltpu.VMEM((RING, RING, TOK, FEAT), BF16),
            pltpu.VMEM((FEAT, FEAT), BF16),
            pltpu.VMEM((OWN, TOK, BLOCK), BF16),
            pltpu.VMEM((n, PAIR, FEAT), BF16),
            pltpu.VMEM((n, PAIR, FEAT), F32),
            pltpu.VMEM((n, 2, HALF, FEAT), BF16),
            pltpu.VMEM((n, 2, HALF, FEAT), BF16),
            pltpu.VMEM((n, 3, SUB, FEAT), BF16),
            pltpu.VMEM((n, SUB, FEAT), F32),
            pltpu.VMEM((n, SUB, FEAT), F32),
            pltpu.VMEM((n, HALF, FEAT), F32),
            pltpu.VMEM((RING, 2, RING, SUB, FEAT), BF16),
            pltpu.VMEM((3 * SLOTS, TOK, BLOCK), BF16),
            pltpu.VMEM((RING * SLOTS, TOK, BLOCK), BF16),
            pltpu.VMEM((3 * SLOTS, TOK, BLOCK), BF16),
            pltpu.VMEM((RING * SLOTS, TOK, BLOCK), BF16),
            pltpu.VMEM((TOK, KEPT), BF16),
            pltpu.VMEM((RING, RING, TOK, KEPT), BF16),
            pltpu.VMEM((RING, RING, TOK, KEPT), BF16),
            pltpu.SemaphoreType.DMA((2 + OWN,)),
            pltpu.SemaphoreType.DMA((COPIES,)),
            pltpu.SemaphoreType.DMA((COPIES,)),
        ],
        compiler_params=pltpu.CompilerParams(
            collective_id=0, has_side_effects=True, vmem_limit_bytes=VMEM),
        name="gram_cross",
    )(kept_blocks, teacher_in, weight, student_in)


def solution(mesh):
    return jax.shard_map(
        local,
        mesh=mesh,
        in_specs=(
            P(("grp", "col"), "row"),
            P("row", ("grp", "col")),
            P(("grp", "col"), "row"),
            P(),
        ),
        out_specs=(P("row", ("grp", "col")), P("row", ("grp", "col"))),
        check_vma=False,
    )
```

```python
import jax
import jax.numpy as jnp
from jax import lax
from jax.experimental import pallas as pl
from jax.experimental.pallas import tpu as pltpu
from jax.sharding import PartitionSpec as P

MESH = pl.DeviceIdType.MESH
F32 = jnp.float32
BF16 = jnp.bfloat16
RING = 4
TOK = 128
PAIR = 2 * TOK
SUB = PAIR // RING
HALF = SUB // 2
FEAT = 768
KEPT = 384
BLOCK = 128
OWN = FEAT // BLOCK
SLOTS = KEPT // BLOCK
ORDER = (0, 1, 3, 2)
CHUNKS = tuple((k, w) for w in (0, 1) for k in ORDER)
INV = 1.0 / 2048
COPIES = 240
RELAYED = (0, 0, 0, 0, 1, 1, 1, 1)
VMEM = 65273856


def wrap(v):
    return lax.rem(v + RING, RING)


def always(body):
    body()


def kernel(kept, x_hbm, w_hbm, s_hbm, gram_ref, cross_ref,
           xg, wv, sblk, part, mine, hopin, both, xin, total, zin, zhalf, tg,
           packx, sx, packz, kin, tile, kr, kc,
           load_sem, send_sem, recv_sem):
    y, row, col = lax.axis_index("grp"), lax.axis_index("row"), lax.axis_index("col")
    zl, x = lax.div(row, RING), lax.rem(row, RING)
    zh, core = lax.div(col, 2), lax.rem(col, 2)
    sib = col + 1 - 2 * core
    far = wrap(col + 2)
    inner = (zl == 1) | (zl == 2)
    outer = jnp.logical_not(inner)

    def to_x(k):
        return (y, zl * RING + wrap(x + k), col)

    def to_y(k):
        return (wrap(y + k), row, col)

    def at_z(z):
        return (y, z * RING + x, col)

    to_far = (y, row, far)
    to_sib = (y, row, sib)
    flip = (zl, y * RING + col, x)
    off_diagonal = row != y * RING + col

    count = [0, 0]
    open_sends = []
    owed = {}
    done = []

    def copy(src, dst, device, recv=None):
        i = count[0]
        count[0] += 1
        if recv is None:
            recv = count[1]
            count[1] += 1
        return pltpu.make_async_remote_copy(
            src_ref=src, dst_ref=dst, send_sem=send_sem.at[i], recv_sem=recv_sem.at[recv],
            device_id=device, device_id_type=MESH)

    def push(src, dst, device, recv=None):
        c = copy(src, dst, device, recv)
        c.start()
        open_sends.append((always, c))
        owed[id(c)] = (always, c)
        return c

    def got(c):
        when, c = owed.pop(id(c))
        when(c.wait_recv)

    loads = [pltpu.make_async_copy(x_hbm, xg.at[y, col], load_sem.at[0])]
    for b in range(OWN):
        loads.append(pltpu.make_async_copy(
            s_hbm.at[:, pl.ds(b * BLOCK, BLOCK)], sblk.at[b], load_sem.at[1 + b]))
    loads.append(pltpu.make_async_copy(w_hbm, wv, load_sem.at[1 + OWN]))
    for c in loads:
        c.start()

    kin[...] = jnp.zeros_like(kin)
    barrier = pltpu.get_barrier_semaphore()
    peers = [to_far, to_sib]
    for k in (1, 2, 3):
        peers += [to_x(k), to_y(k), at_z(wrap(zl + k))]
    for p in peers:
        pl.semaphore_signal(barrier, inc=1, device_id=p, device_id_type=MESH)

    @pl.when(off_diagonal)
    def _():
        pl.semaphore_signal(barrier, inc=1, device_id=flip, device_id_type=MESH)

    pl.semaphore_wait(barrier, len(peers) + off_diagonal.astype(jnp.int32))

    class Gather:
        def __init__(self, buf, own):
            self.buf = buf
            slot = buf.at[y, col]
            self.far = push(own, slot, to_far)
            self.sib = {(0, 0): push(own, slot, to_sib)}
            self.near = {(k, 0): push(own, slot, to_y(k)) for k in ORDER[1:]}

        def spread(self):
            got(self.far)
            piece = self.buf.at[y, far]
            self.sib[0, 1] = push(piece, piece, to_sib)
            for k in ORDER[1:]:
                self.near[k, 1] = push(piece, piece, to_y(k))

        def hand(self, k, w):
            got(self.near[k, w])
            piece = self.buf.at[wrap(y - k), far if w else col]
            self.sib[k, w] = push(piece, piece, to_sib)

        def ready(self, k, w):
            got(self.sib[k, w])

    loads[0].wait()
    gx = Gather(xg, xg.at[y, col])

    for b in range(OWN):
        loads[1 + b].wait()
    student = []
    for k in (1, 3, 2, 0):
        xt = wrap(x + k)
        for j in range(SLOTS):
            pick = jnp.int32(0)
            for zt in range(RING):
                p = kept[(zt * RING + xt) * SLOTS + j] - row * OWN
                pick = jnp.where((p >= 0) & (p < OWN), p, pick)
            if k == 0:
                sx[x * SLOTS + j] = sblk[pick]
            else:
                packx[(k - 1) * SLOTS + j] = sblk[pick]
        if k:
            student.append(push(packx.at[pl.ds((k - 1) * SLOTS, SLOTS)],
                                sx.at[pl.ds(x * SLOTS, SLOTS)], to_x(k)))

    def linked(src, dst):
        gap = dst - src
        return (gap == 1) | (gap == -1) | ((src == 2) & (dst == 0)) | ((src == 1) & (dst == 3))

    packs = []

    def send_packs():
        for c in student:
            got(c)
        for k in range(RING):
            zt = wrap(zl + k)
            for j in range(SLOTS):
                p = kept[(zt * RING + x) * SLOTS + j]
                block = sx[lax.rem(lax.div(p, OWN), RING) * SLOTS + j]
                if k == 0:
                    kin[zl * SLOTS + j] = block
                else:
                    packz[(k - 1) * SLOTS + j] = block
            if k:
                c = copy(packz.at[pl.ds((k - 1) * SLOTS, SLOTS)],
                         kin.at[pl.ds(zl * SLOTS, SLOTS)], at_z(zt))
                packs.append((k, c))
                goes = pl.when(linked(zl, zt))
                goes(c.start)
                open_sends.append((goes, c))
                owed[id(c)] = (pl.when(linked(wrap(zl - k), zl)), c)

    def make_tile():
        for k, c in packs:
            got(c)
        for j in range(SLOTS):
            p = kept[row * SLOTS + j]
            tile[:, j * BLOCK:(j + 1) * BLOCK] = kin[lax.div(p, RING * OWN) * SLOTS + j]
        kr[y, col] = tile[...]

    hop, rsx, rsz, mid, agz, agx, fwd = {}, {}, {}, {}, {}, {}, {}
    place = [(wrap(y - k), lax.rem(zh + w, 2)) for k, w in CHUNKS]

    def stage_a(i):
        k, w = CHUNKS[i]
        gx.ready(k, w)
        q, h = place[i]
        lhs = xg[q, pl.ds(2 * h, 2)].reshape(PAIR, FEAT)
        out = jnp.dot(lhs, wv[...], preferred_element_type=F32)
        part[i] = out.astype(BF16)
        mine[i] = out
        if not RELAYED[i]:
            for n, k in enumerate((2, 1, 3)):
                rsx[i, n, 0] = push(part.at[i, pl.ds(wrap(x + k) * SUB, SUB)], xin.at[i, n], to_x(k))
            return
        for n, k in enumerate((1, 3)):
            hop[i, n] = push(part.at[i, pl.ds(wrap(x + 2) * SUB + n * HALF, HALF)], hopin.at[i, n], to_x(k))
        for n, k in enumerate((1, 3)):
            lo = (1 - n) * HALF
            rsx[i, n, 0] = push(part.at[i, pl.ds(wrap(x + k) * SUB + lo, HALF)],
                                xin.at[i, n, pl.ds(lo, HALF)], to_x(k))

    def stage_h(i):
        for n, k in enumerate((1, 3)):
            got(hop[i, n])
            rows = pl.ds(wrap(x + k) * SUB + n * HALF, HALF)
            both[i, n] = (mine[i, rows] + hopin[i, n].astype(F32)).astype(BF16)
            rsx[i, n, 1] = push(both.at[i, n], xin.at[i, n, pl.ds(n * HALF, HALF)], to_x(k))

    def stage_b(i):
        own = mine[i, pl.ds(x * SUB, SUB)]
        for n in range(2 if RELAYED[i] else 3):
            for m in range(2 if RELAYED[i] else 1):
                got(rsx[i, n, m])
        if not RELAYED[i]:
            own = own + xin[i, 2].astype(F32)
        total[i] = own + (xin[i, 0].astype(F32) + xin[i, 1].astype(F32))
        c = copy(total.at[i], zin.at[i], at_z(jnp.where(zl < 2, 1, 2)))
        pl.when(outer)(c.start)
        open_sends.append((pl.when(outer), c))
        owed[id(c)] = (pl.when(inner), c)
        rsz[i] = c

    def stage_c(i):
        c = copy(total.at[i, pl.ds(lax.rem(zl, 2) * HALF, HALF)], zhalf.at[i], at_z(3 - zl))
        mid[i] = c
        owed[id(c)] = (pl.when(inner), c)
        open_sends.append((pl.when(inner), c))

        got(rsz[i])

        @pl.when(inner)
        def _():
            total[i] = total[i] + zin[i]
            c.start()

    def stage_d(i):
        h = lax.rem(zl + 1, 2)
        rows = pl.ds(h * HALF, HALF)
        q, g = place[i]
        piece = tg.at[q, g, x, rows]
        base = count[1]
        count[1] += 2
        cs = [copy(piece, piece, at_z(wrap(zl + k)), base + h) for k in (1, 2, 3)]
        agz[i] = []
        for n in (0, 1):
            c = pltpu.make_async_remote_copy(
                src_ref=tg.at[q, g, x, pl.ds(n * HALF, HALF)],
                dst_ref=tg.at[q, g, x, pl.ds(n * HALF, HALF)], send_sem=send_sem.at[0],
                recv_sem=recv_sem.at[base + n], device_id=to_sib, device_id_type=MESH)
            owed[id(c)] = (pl.when(zl != n + 1), c)
            agz[i].append(c)
        for c in cs:
            open_sends.append((pl.when(inner), c))

        got(mid[i])

        @pl.when(inner)
        def _():
            tg[q, g, x, rows] = (total[i, rows] + zhalf[i]).astype(BF16)
            for c in cs:
                c.start()

    def stage_e(i):
        q, g = place[i]
        for c in agz[i]:
            got(c)
        piece = tg.at[q, g, x]
        for k in (1, 3):
            agx[i, k] = push(piece, piece, to_x(k))

    def stage_f(i):
        q, g = place[i]
        for k, lo in ((1, 0), (3, HALF)):
            got(agx[i, k])
            piece = tg.at[q, g, wrap(x - k), pl.ds(lo, HALF)]
            fwd[i, k] = push(piece, piece, to_x(k))

    def stage_g(i):
        for k in (1, 3):
            got(fwd[i, k])
        q, g = place[i]
        lhs = kr[q, pl.ds(2 * g, 2)].reshape(PAIR, KEPT)
        rhs = tg[q, g].reshape(PAIR, FEAT)
        out = lax.dot_general(lhs, rhs, (((0,), (0,)), ((), ())), preferred_element_type=F32)
        done.append(i)
        if len(done) == 1:
            cross_ref[...] = out
        elif len(done) < len(CHUNKS):
            cross_ref[...] += out
        else:
            cross_ref[...] = (cross_ref[...] + out) * INV

    def tile_out():
        make_tile()
        gather["k"] = Gather(kr, tile)
        c = copy(tile, kc.at[col, y], flip)
        pl.when(off_diagonal)(c.start)
        open_sends.append((pl.when(off_diagonal), c))
        owed[id(c)] = (pl.when(off_diagonal), c)
        share.append(c)

        @pl.when(jnp.logical_not(off_diagonal))
        def _():
            kc[x, zl] = tile[...]

    def hand(which, i):
        gather[which].hand(*CHUNKS[i])

    def spread(which):
        gather[which].spread()

    def share_here():
        if share:
            got(share.pop())
        return kc.at[x, zl]

    def share_z(k):
        piece = share_here()
        colz[k] = push(piece, piece, at_z(wrap(zl + k)))

    def share_x(k):
        if k:
            got(colz[k])
            piece = kc.at[x, wrap(zl - k)]
        else:
            piece = share_here()
        for d in (1, 3):
            colx[k, d] = push(piece, piece, to_x(d))

    def share_fwd(h):
        for k, d in ((2 * h, 1), (2 * h + 1, 3)):
            for e in (1, 3):
                got(colx[k, e])
            piece = kc.at[wrap(x - d), wrap(zl - k)]
            colf.append(push(piece, piece, to_x(d)))

    def k_ready():
        for k, w in CHUNKS:
            gather["k"].ready(k, w)

    def gram():
        for c in colf:
            got(c)

        def gram_body(j, carry):
            lhs = kr[:, j].reshape(RING * TOK, KEPT)
            rhs = kc[j].reshape(RING * TOK, KEPT)
            gram_ref[...] += lax.dot_general(lhs, rhs, (((0,), (0,)), ((), ())), preferred_element_type=F32)
            return carry

        gram_ref[...] = jnp.zeros_like(gram_ref)
        lax.fori_loop(0, RING, gram_body, 0)
        gram_ref[...] = gram_ref[...] * INV

    gather, share, colz, colx, colf = {"x": gx}, [], {}, {}, []
    A, H, B, C, D, E, F, G = stage_a, stage_h, stage_b, stage_c, stage_d, stage_e, stage_f, stage_g
    steps = (
        (loads[1 + OWN].wait,), (A, 0), (hand, "x", 1), (hand, "x", 2), (send_packs,), (A, 1),
        (spread, "x"), (B, 0), (A, 2), (tile_out,), (hand, "x", 5), (hand, "x", 6), (B, 1), (A, 5),
        (C, 0), (A, 4), (hand, "x", 7), (H, 5), (B, 2), (A, 7), (D, 0), (spread, "k"), (hand, "x", 3),
        (hand, "k", 3), (H, 4), (hand, "k", 1), (B, 5), (C, 1), (H, 7), (A, 6), (A, 3), (hand, "k", 6),
        (B, 4), (C, 2), (E, 0), (D, 1), (hand, "k", 7), (C, 5), (D, 2), (H, 6), (B, 7), (hand, "k", 5),
        (E, 1), (share_z, 1), (C, 4), (share_x, 0), (F, 0), (share_z, 3), (share_z, 2), (B, 3), (F, 1),
        (E, 2), (hand, "k", 2), (share_x, 1), (C, 7), (D, 4), (D, 5), (share_x, 3), (F, 2),
        (share_fwd, 0), (B, 6), (share_x, 2), (D, 7), (E, 4), (C, 3), (E, 5), (C, 6), (k_ready,),
        (share_fwd, 1), (E, 7), (D, 3), (F, 5), (D, 6), (F, 4), (E, 3), (G, 2), (E, 6), (G, 0), (G, 1),
        (G, 5), (F, 3), (G, 4), (F, 7), (F, 6), (gram,), (G, 3), (G, 7), (G, 6),
    )
    for step, *args in steps:
        step(*args)

    for when, c in tuple(owed.values()):
        when(c.wait_recv)
    for when, c in open_sends:
        when(c.wait_send)


def local(teacher_in, weight, student_in, kept_blocks):
    vmem = pl.BlockSpec(memory_space=pltpu.VMEM)
    hbm = pl.BlockSpec(memory_space=pltpu.HBM)
    n = len(CHUNKS)
    return pl.pallas_call(
        kernel,
        out_shape=(jax.ShapeDtypeStruct((KEPT, KEPT), F32),
                   jax.ShapeDtypeStruct((KEPT, FEAT), F32)),
        in_specs=[pl.BlockSpec(memory_space=pltpu.SMEM), hbm, hbm, hbm],
        out_specs=(vmem, vmem),
        scratch_shapes=[
            pltpu.VMEM((RING, RING, TOK, FEAT), BF16),
            pltpu.VMEM((FEAT, FEAT), BF16),
            pltpu.VMEM((OWN, TOK, BLOCK), BF16),
            pltpu.VMEM((n, PAIR, FEAT), BF16),
            pltpu.VMEM((n, PAIR, FEAT), F32),
            pltpu.VMEM((n, 2, HALF, FEAT), BF16),
            pltpu.VMEM((n, 2, HALF, FEAT), BF16),
            pltpu.VMEM((n, 3, SUB, FEAT), BF16),
            pltpu.VMEM((n, SUB, FEAT), F32),
            pltpu.VMEM((n, SUB, FEAT), F32),
            pltpu.VMEM((n, HALF, FEAT), F32),
            pltpu.VMEM((RING, 2, RING, SUB, FEAT), BF16),
            pltpu.VMEM((3 * SLOTS, TOK, BLOCK), BF16),
            pltpu.VMEM((RING * SLOTS, TOK, BLOCK), BF16),
            pltpu.VMEM((3 * SLOTS, TOK, BLOCK), BF16),
            pltpu.VMEM((RING * SLOTS, TOK, BLOCK), BF16),
            pltpu.VMEM((TOK, KEPT), BF16),
            pltpu.VMEM((RING, RING, TOK, KEPT), BF16),
            pltpu.VMEM((RING, RING, TOK, KEPT), BF16),
            pltpu.SemaphoreType.DMA((2 + OWN,)),
            pltpu.SemaphoreType.DMA((COPIES,)),
            pltpu.SemaphoreType.DMA((COPIES,)),
        ],
        compiler_params=pltpu.CompilerParams(
            collective_id=0, has_side_effects=True, vmem_limit_bytes=VMEM),
        name="gram_cross",
    )(kept_blocks, teacher_in, weight, student_in)


def solution(mesh):
    return jax.shard_map(
        local,
        mesh=mesh,
        in_specs=(
            P(("grp", "col"), "row"),
            P("row", ("grp", "col")),
            P(("grp", "col"), "row"),
            P(),
        ),
        out_specs=(P("row", ("grp", "col")), P("row", ("grp", "col"))),
        check_vma=False,
    )
```

```python
import jax
import jax.numpy as jnp
from jax import lax
from jax.experimental import pallas as pl
from jax.experimental.pallas import tpu as pltpu
from jax.sharding import PartitionSpec as P

MESH = pl.DeviceIdType.MESH
F32 = jnp.float32
BF16 = jnp.bfloat16
RING = 4
TOK = 128
PAIR = 2 * TOK
SUB = PAIR // RING
HALF = SUB // 2
FEAT = 768
KEPT = 384
BLOCK = 128
OWN = FEAT // BLOCK
SLOTS = KEPT // BLOCK
ORDER = (0, 1, 3, 2)
CHUNKS = tuple((k, w) for w in (0, 1) for k in ORDER)
INV = 1.0 / 2048
COPIES = 240
RELAYED = (0, 0, 0, 0, 1, 1, 1, 1)
VMEM = 65273856


def wrap(v):
    return lax.rem(v + RING, RING)


def always(body):
    body()


def kernel(kept, x_hbm, w_hbm, s_hbm, gram_ref, cross_ref,
           xg, wv, sblk, part, mine, hopin, both, xin, total, zin, zhalf, tg,
           packx, sx, packz, kin, tile, kr, kc,
           load_sem, send_sem, recv_sem):
    y, row, col = lax.axis_index("grp"), lax.axis_index("row"), lax.axis_index("col")
    zl, x = lax.div(row, RING), lax.rem(row, RING)
    zh, core = lax.div(col, 2), lax.rem(col, 2)
    sib = col + 1 - 2 * core
    far = wrap(col + 2)
    inner = (zl == 1) | (zl == 2)
    outer = jnp.logical_not(inner)

    def to_x(k):
        return (y, zl * RING + wrap(x + k), col)

    def to_y(k):
        return (wrap(y + k), row, col)

    def at_z(z):
        return (y, z * RING + x, col)

    to_far = (y, row, far)
    to_sib = (y, row, sib)
    flip = (zl, y * RING + col, x)
    off_diagonal = row != y * RING + col

    count = [0, 0]
    open_sends = []
    owed = {}
    done = []

    def copy(src, dst, device, recv=None):
        i = count[0]
        count[0] += 1
        if recv is None:
            recv = count[1]
            count[1] += 1
        return pltpu.make_async_remote_copy(
            src_ref=src, dst_ref=dst, send_sem=send_sem.at[i], recv_sem=recv_sem.at[recv],
            device_id=device, device_id_type=MESH)

    def push(src, dst, device, recv=None):
        c = copy(src, dst, device, recv)
        c.start()
        open_sends.append((always, c))
        owed[id(c)] = (always, c)
        return c

    def got(c):
        when, c = owed.pop(id(c))
        when(c.wait_recv)

    loads = [pltpu.make_async_copy(x_hbm, xg.at[y, col], load_sem.at[0])]
    for b in range(OWN):
        loads.append(pltpu.make_async_copy(
            s_hbm.at[:, pl.ds(b * BLOCK, BLOCK)], sblk.at[b], load_sem.at[1 + b]))
    loads.append(pltpu.make_async_copy(w_hbm, wv, load_sem.at[1 + OWN]))
    for c in loads:
        c.start()

    kin[...] = jnp.zeros_like(kin)
    barrier = pltpu.get_barrier_semaphore()
    peers = [to_far, to_sib]
    for k in (1, 2, 3):
        peers += [to_x(k), to_y(k), at_z(wrap(zl + k))]
    for p in peers:
        pl.semaphore_signal(barrier, inc=1, device_id=p, device_id_type=MESH)

    @pl.when(off_diagonal)
    def _():
        pl.semaphore_signal(barrier, inc=1, device_id=flip, device_id_type=MESH)

    pl.semaphore_wait(barrier, len(peers) + off_diagonal.astype(jnp.int32))

    class Gather:
        def __init__(self, buf, own):
            self.buf = buf
            slot = buf.at[y, col]
            self.far = push(own, slot, to_far)
            self.sib = {(0, 0): push(own, slot, to_sib)}
            self.near = {(k, 0): push(own, slot, to_y(k)) for k in ORDER[1:]}

        def spread(self):
            got(self.far)
            piece = self.buf.at[y, far]
            self.sib[0, 1] = push(piece, piece, to_sib)
            for k in ORDER[1:]:
                self.near[k, 1] = push(piece, piece, to_y(k))

        def hand(self, k, w):
            got(self.near[k, w])
            piece = self.buf.at[wrap(y - k), far if w else col]
            self.sib[k, w] = push(piece, piece, to_sib)

        def ready(self, k, w):
            got(self.sib[k, w])

    loads[0].wait()
    gx = Gather(xg, xg.at[y, col])

    for b in range(OWN):
        loads[1 + b].wait()
    student = []
    for k in (2, 1, 3, 0):
        xt = wrap(x + k)
        for j in range(SLOTS):
            pick = jnp.int32(0)
            for zt in range(RING):
                p = kept[(zt * RING + xt) * SLOTS + j] - row * OWN
                pick = jnp.where((p >= 0) & (p < OWN), p, pick)
            if k == 0:
                sx[x * SLOTS + j] = sblk[pick]
            else:
                packx[(k - 1) * SLOTS + j] = sblk[pick]
        if k:
            student.append(push(packx.at[pl.ds((k - 1) * SLOTS, SLOTS)],
                                sx.at[pl.ds(x * SLOTS, SLOTS)], to_x(k)))

    def linked(src, dst):
        gap = dst - src
        return (gap == 1) | (gap == -1) | ((src == 2) & (dst == 0)) | ((src == 1) & (dst == 3))

    packs = []

    def send_packs():
        for c in student:
            got(c)
        for k in range(RING):
            zt = wrap(zl + k)
            for j in range(SLOTS):
                p = kept[(zt * RING + x) * SLOTS + j]
                block = sx[lax.rem(lax.div(p, OWN), RING) * SLOTS + j]
                if k == 0:
                    kin[zl * SLOTS + j] = block
                else:
                    packz[(k - 1) * SLOTS + j] = block
            if k:
                c = copy(packz.at[pl.ds((k - 1) * SLOTS, SLOTS)],
                         kin.at[pl.ds(zl * SLOTS, SLOTS)], at_z(zt))
                packs.append((k, c))
                goes = pl.when(linked(zl, zt))
                goes(c.start)
                open_sends.append((goes, c))
                owed[id(c)] = (pl.when(linked(wrap(zl - k), zl)), c)

    def make_tile():
        for k, c in packs:
            got(c)
        for j in range(SLOTS):
            p = kept[row * SLOTS + j]
            tile[:, j * BLOCK:(j + 1) * BLOCK] = kin[lax.div(p, RING * OWN) * SLOTS + j]
        kr[y, col] = tile[...]

    hop, rsx, rsz, mid, agz, agx, fwd = {}, {}, {}, {}, {}, {}, {}
    place = [(wrap(y - k), lax.rem(zh + w, 2)) for k, w in CHUNKS]

    def stage_a(i):
        k, w = CHUNKS[i]
        gx.ready(k, w)
        q, h = place[i]
        lhs = xg[q, pl.ds(2 * h, 2)].reshape(PAIR, FEAT)
        out = jnp.dot(lhs, wv[...], preferred_element_type=F32)
        part[i] = out.astype(BF16)
        mine[i] = out
        if not RELAYED[i]:
            for n, k in enumerate((2, 1, 3)):
                rsx[i, n, 0] = push(part.at[i, pl.ds(wrap(x + k) * SUB, SUB)], xin.at[i, n], to_x(k))
            return
        for n, k in enumerate((1, 3)):
            hop[i, n] = push(part.at[i, pl.ds(wrap(x + 2) * SUB + n * HALF, HALF)], hopin.at[i, n], to_x(k))
        for n, k in enumerate((1, 3)):
            lo = (1 - n) * HALF
            rsx[i, n, 0] = push(part.at[i, pl.ds(wrap(x + k) * SUB + lo, HALF)],
                                xin.at[i, n, pl.ds(lo, HALF)], to_x(k))

    def stage_h(i):
        for n, k in enumerate((1, 3)):
            got(hop[i, n])
            rows = pl.ds(wrap(x + k) * SUB + n * HALF, HALF)
            both[i, n] = (mine[i, rows] + hopin[i, n].astype(F32)).astype(BF16)
            rsx[i, n, 1] = push(both.at[i, n], xin.at[i, n, pl.ds(n * HALF, HALF)], to_x(k))

    def stage_b(i):
        own = mine[i, pl.ds(x * SUB, SUB)]
        for n in range(2 if RELAYED[i] else 3):
            for m in range(2 if RELAYED[i] else 1):
                got(rsx[i, n, m])
        if not RELAYED[i]:
            own = own + xin[i, 2].astype(F32)
        total[i] = own + (xin[i, 0].astype(F32) + xin[i, 1].astype(F32))
        c = copy(total.at[i], zin.at[i], at_z(jnp.where(zl < 2, 1, 2)))
        pl.when(outer)(c.start)
        open_sends.append((pl.when(outer), c))
        owed[id(c)] = (pl.when(inner), c)
        rsz[i] = c

    def stage_c(i):
        c = copy(total.at[i, pl.ds(lax.rem(zl, 2) * HALF, HALF)], zhalf.at[i], at_z(3 - zl))
        mid[i] = c
        owed[id(c)] = (pl.when(inner), c)
        open_sends.append((pl.when(inner), c))

        got(rsz[i])

        @pl.when(inner)
        def _():
            total[i] = total[i] + zin[i]
            c.start()

    def stage_d(i):
        h = lax.rem(zl + 1, 2)
        rows = pl.ds(h * HALF, HALF)
        q, g = place[i]
        piece = tg.at[q, g, x, rows]
        base = count[1]
        count[1] += 2
        cs = [copy(piece, piece, at_z(wrap(zl + k)), base + h) for k in (2, 1, 3)]
        agz[i] = []
        for n in (0, 1):
            c = pltpu.make_async_remote_copy(
                src_ref=tg.at[q, g, x, pl.ds(n * HALF, HALF)],
                dst_ref=tg.at[q, g, x, pl.ds(n * HALF, HALF)], send_sem=send_sem.at[0],
                recv_sem=recv_sem.at[base + n], device_id=to_sib, device_id_type=MESH)
            owed[id(c)] = (pl.when(zl != n + 1), c)
            agz[i].append(c)
        for c in cs:
            open_sends.append((pl.when(inner), c))

        got(mid[i])

        @pl.when(inner)
        def _():
            tg[q, g, x, rows] = (total[i, rows] + zhalf[i]).astype(BF16)
            for c in cs:
                c.start()

    def stage_e(i):
        q, g = place[i]
        for c in agz[i]:
            got(c)
        piece = tg.at[q, g, x]
        for k in (1, 3):
            agx[i, k] = push(piece, piece, to_x(k))

    def stage_f(i):
        q, g = place[i]
        for k, lo in ((1, 0), (3, HALF)):
            got(agx[i, k])
            piece = tg.at[q, g, wrap(x - k), pl.ds(lo, HALF)]
            fwd[i, k] = push(piece, piece, to_x(k))

    def stage_g(i):
        for k in (1, 3):
            got(fwd[i, k])
        q, g = place[i]
        lhs = kr[q, pl.ds(2 * g, 2)].reshape(PAIR, KEPT)
        rhs = tg[q, g].reshape(PAIR, FEAT)
        out = lax.dot_general(lhs, rhs, (((0,), (0,)), ((), ())), preferred_element_type=F32)
        done.append(i)
        if len(done) == 1:
            cross_ref[...] = out
        elif len(done) < len(CHUNKS):
            cross_ref[...] += out
        else:
            cross_ref[...] = (cross_ref[...] + out) * INV

    def tile_out():
        make_tile()
        gather["k"] = Gather(kr, tile)
        c = copy(tile, kc.at[col, y], flip)
        pl.when(off_diagonal)(c.start)
        open_sends.append((pl.when(off_diagonal), c))
        owed[id(c)] = (pl.when(off_diagonal), c)
        share.append(c)

        @pl.when(jnp.logical_not(off_diagonal))
        def _():
            kc[x, zl] = tile[...]

    def hand(which, i):
        gather[which].hand(*CHUNKS[i])

    def spread(which):
        gather[which].spread()

    def share_here():
        if share:
            got(share.pop())
        return kc.at[x, zl]

    def share_z(k):
        piece = share_here()
        colz[k] = push(piece, piece, at_z(wrap(zl + k)))

    def share_x(k):
        if k:
            got(colz[k])
            piece = kc.at[x, wrap(zl - k)]
        else:
            piece = share_here()
        for d in (1, 3):
            colx[k, d] = push(piece, piece, to_x(d))

    def share_fwd(h):
        for k, d in ((2 * h, 1), (2 * h + 1, 3)):
            for e in (1, 3):
                got(colx[k, e])
            piece = kc.at[wrap(x - d), wrap(zl - k)]
            colf.append(push(piece, piece, to_x(d)))

    def k_ready():
        for k, w in CHUNKS:
            gather["k"].ready(k, w)

    def gram():
        for c in colf:
            got(c)

        def gram_body(j, carry):
            lhs = kr[:, j].reshape(RING * TOK, KEPT)
            rhs = kc[j].reshape(RING * TOK, KEPT)
            gram_ref[...] += lax.dot_general(lhs, rhs, (((0,), (0,)), ((), ())), preferred_element_type=F32)
            return carry

        gram_ref[...] = jnp.zeros_like(gram_ref)
        lax.fori_loop(0, RING, gram_body, 0)
        gram_ref[...] = gram_ref[...] * INV

    gather, share, colz, colx, colf = {"x": gx}, [], {}, {}, []
    A, H, B, C, D, E, F, G = stage_a, stage_h, stage_b, stage_c, stage_d, stage_e, stage_f, stage_g
    steps = (
        (loads[1 + OWN].wait,), (A, 0), (hand, "x", 1), (hand, "x", 2), (send_packs,), (A, 1),
        (spread, "x"), (B, 0), (A, 2), (tile_out,), (hand, "x", 5), (hand, "x", 6), (B, 1), (A, 5),
        (C, 0), (A, 4), (hand, "x", 7), (H, 5), (B, 2), (A, 7), (D, 0), (spread, "k"), (hand, "x", 3),
        (hand, "k", 3), (H, 4), (hand, "k", 1), (B, 5), (C, 1), (H, 7), (A, 6), (A, 3), (hand, "k", 6),
        (B, 4), (C, 2), (E, 0), (D, 1), (hand, "k", 7), (C, 5), (D, 2), (H, 6), (B, 7), (hand, "k", 5),
        (E, 1), (share_z, 1), (C, 4), (share_x, 0), (F, 0), (share_z, 3), (share_z, 2), (B, 3), (F, 1),
        (E, 2), (hand, "k", 2), (share_x, 1), (C, 7), (D, 4), (D, 5), (share_x, 3), (F, 2),
        (share_fwd, 0), (B, 6), (share_x, 2), (D, 7), (E, 4), (C, 3), (E, 5), (C, 6), (k_ready,),
        (share_fwd, 1), (E, 7), (D, 3), (F, 5), (D, 6), (F, 4), (E, 3), (G, 2), (E, 6), (G, 0), (G, 1),
        (G, 5), (F, 3), (G, 4), (F, 7), (F, 6), (gram,), (G, 3), (G, 7), (G, 6),
    )
    for step, *args in steps:
        step(*args)

    for when, c in tuple(owed.values()):
        when(c.wait_recv)
    for when, c in open_sends:
        when(c.wait_send)


def local(teacher_in, weight, student_in, kept_blocks):
    vmem = pl.BlockSpec(memory_space=pltpu.VMEM)
    hbm = pl.BlockSpec(memory_space=pltpu.HBM)
    n = len(CHUNKS)
    return pl.pallas_call(
        kernel,
        out_shape=(jax.ShapeDtypeStruct((KEPT, KEPT), F32),
                   jax.ShapeDtypeStruct((KEPT, FEAT), F32)),
        in_specs=[pl.BlockSpec(memory_space=pltpu.SMEM), hbm, hbm, hbm],
        out_specs=(vmem, vmem),
        scratch_shapes=[
            pltpu.VMEM((RING, RING, TOK, FEAT), BF16),
            pltpu.VMEM((FEAT, FEAT), BF16),
            pltpu.VMEM((OWN, TOK, BLOCK), BF16),
            pltpu.VMEM((n, PAIR, FEAT), BF16),
            pltpu.VMEM((n, PAIR, FEAT), F32),
            pltpu.VMEM((n, 2, HALF, FEAT), BF16),
            pltpu.VMEM((n, 2, HALF, FEAT), BF16),
            pltpu.VMEM((n, 3, SUB, FEAT), BF16),
            pltpu.VMEM((n, SUB, FEAT), F32),
            pltpu.VMEM((n, SUB, FEAT), F32),
            pltpu.VMEM((n, HALF, FEAT), F32),
            pltpu.VMEM((RING, 2, RING, SUB, FEAT), BF16),
            pltpu.VMEM((3 * SLOTS, TOK, BLOCK), BF16),
            pltpu.VMEM((RING * SLOTS, TOK, BLOCK), BF16),
            pltpu.VMEM((3 * SLOTS, TOK, BLOCK), BF16),
            pltpu.VMEM((RING * SLOTS, TOK, BLOCK), BF16),
            pltpu.VMEM((TOK, KEPT), BF16),
            pltpu.VMEM((RING, RING, TOK, KEPT), BF16),
            pltpu.VMEM((RING, RING, TOK, KEPT), BF16),
            pltpu.SemaphoreType.DMA((2 + OWN,)),
            pltpu.SemaphoreType.DMA((COPIES,)),
            pltpu.SemaphoreType.DMA((COPIES,)),
        ],
        compiler_params=pltpu.CompilerParams(
            collective_id=0, has_side_effects=True, vmem_limit_bytes=VMEM),
        name="gram_cross",
    )(kept_blocks, teacher_in, weight, student_in)


def solution(mesh):
    return jax.shard_map(
        local,
        mesh=mesh,
        in_specs=(
            P(("grp", "col"), "row"),
            P("row", ("grp", "col")),
            P(("grp", "col"), "row"),
            P(),
        ),
        out_specs=(P("row", ("grp", "col")), P("row", ("grp", "col"))),
        check_vma=False,
    )
```

```python
import jax
import jax.numpy as jnp
from jax import lax
from jax.experimental import pallas as pl
from jax.experimental.pallas import tpu as pltpu
from jax.sharding import PartitionSpec as P

MESH = pl.DeviceIdType.MESH
F32 = jnp.float32
BF16 = jnp.bfloat16
RING = 4
TOK = 128
PAIR = 2 * TOK
SUB = PAIR // RING
HALF = SUB // 2
FEAT = 768
KEPT = 384
BLOCK = 128
OWN = FEAT // BLOCK
SLOTS = KEPT // BLOCK
ORDER = (0, 1, 3, 2)
CHUNKS = tuple((k, w) for w in (0, 1) for k in ORDER)
INV = 1.0 / 2048
COPIES = 240
RELAYED = (0, 0, 0, 0, 1, 1, 1, 1)
VMEM = 65273856


def wrap(v):
    return lax.rem(v + RING, RING)


def always(body):
    body()


def kernel(kept, x_hbm, w_hbm, s_hbm, gram_ref, cross_ref,
           xg, wv, sblk, part, mine, hopin, both, xin, total, zin, zhalf, tg,
           packx, sx, packz, kin, tile, kr, kc,
           load_sem, send_sem, recv_sem):
    y, row, col = lax.axis_index("grp"), lax.axis_index("row"), lax.axis_index("col")
    zl, x = lax.div(row, RING), lax.rem(row, RING)
    zh, core = lax.div(col, 2), lax.rem(col, 2)
    sib = col + 1 - 2 * core
    far = wrap(col + 2)
    inner = (zl == 1) | (zl == 2)
    outer = jnp.logical_not(inner)

    def to_x(k):
        return (y, zl * RING + wrap(x + k), col)

    def to_y(k):
        return (wrap(y + k), row, col)

    def at_z(z):
        return (y, z * RING + x, col)

    to_far = (y, row, far)
    to_sib = (y, row, sib)
    flip = (zl, y * RING + col, x)
    off_diagonal = row != y * RING + col

    count = [0, 0]
    open_sends = []
    owed = {}
    done = []

    def copy(src, dst, device, recv=None):
        i = count[0]
        count[0] += 1
        if recv is None:
            recv = count[1]
            count[1] += 1
        return pltpu.make_async_remote_copy(
            src_ref=src, dst_ref=dst, send_sem=send_sem.at[i], recv_sem=recv_sem.at[recv],
            device_id=device, device_id_type=MESH)

    def push(src, dst, device, recv=None):
        c = copy(src, dst, device, recv)
        c.start()
        open_sends.append((always, c))
        owed[id(c)] = (always, c)
        return c

    def got(c):
        when, c = owed.pop(id(c))
        when(c.wait_recv)

    barrier = pltpu.get_barrier_semaphore()
    peers = [to_far, to_sib] + [f(k) for f in (to_x, to_y) for k in (1, 2, 3)]
    for p in peers:
        pl.semaphore_signal(barrier, inc=1, device_id=p, device_id_type=MESH)

    @pl.when(off_diagonal)
    def _():
        pl.semaphore_signal(barrier, inc=1, device_id=flip, device_id_type=MESH)

    loads = [pltpu.make_async_copy(x_hbm, xg.at[y, col], load_sem.at[0])]
    for b in range(OWN):
        loads.append(pltpu.make_async_copy(
            s_hbm.at[:, pl.ds(b * BLOCK, BLOCK)], sblk.at[b], load_sem.at[1 + b]))
    loads.append(pltpu.make_async_copy(w_hbm, wv, load_sem.at[1 + OWN]))
    for c in loads:
        c.start()

    kin[...] = jnp.zeros_like(kin)
    for k in (1, 2, 3):
        pl.semaphore_signal(barrier, inc=1, device_id=at_z(wrap(zl + k)), device_id_type=MESH)
    pl.semaphore_wait(barrier, len(peers) + 3 + off_diagonal.astype(jnp.int32))

    class Gather:
        def __init__(self, buf, own):
            self.buf = buf
            slot = buf.at[y, col]
            self.far = push(own, slot, to_far)
            self.sib = {(0, 0): push(own, slot, to_sib)}
            self.near = {(k, 0): push(own, slot, to_y(k)) for k in ORDER[1:]}

        def spread(self):
            got(self.far)
            piece = self.buf.at[y, far]
            self.sib[0, 1] = push(piece, piece, to_sib)
            for k in ORDER[1:]:
                self.near[k, 1] = push(piece, piece, to_y(k))

        def hand(self, k, w):
            got(self.near[k, w])
            piece = self.buf.at[wrap(y - k), far if w else col]
            self.sib[k, w] = push(piece, piece, to_sib)

        def ready(self, k, w):
            got(self.sib[k, w])

    loads[0].wait()
    gx = Gather(xg, xg.at[y, col])

    for b in range(OWN):
        loads[1 + b].wait()
    student = []
    for k in (1, 3, 2, 0):
        xt = wrap(x + k)
        for j in range(SLOTS):
            pick = jnp.int32(0)
            for zt in range(RING):
                p = kept[(zt * RING + xt) * SLOTS + j] - row * OWN
                pick = jnp.where((p >= 0) & (p < OWN), p, pick)
            if k == 0:
                sx[x * SLOTS + j] = sblk[pick]
            else:
                packx[(k - 1) * SLOTS + j] = sblk[pick]
        if k:
            student.append(push(packx.at[pl.ds((k - 1) * SLOTS, SLOTS)],
                                sx.at[pl.ds(x * SLOTS, SLOTS)], to_x(k)))

    def linked(src, dst):
        gap = dst - src
        return (gap == 1) | (gap == -1) | ((src == 2) & (dst == 0)) | ((src == 1) & (dst == 3))

    packs = []

    def send_packs():
        for c in student:
            got(c)
        for k in range(RING):
            zt = wrap(zl + k)
            for j in range(SLOTS):
                p = kept[(zt * RING + x) * SLOTS + j]
                block = sx[lax.rem(lax.div(p, OWN), RING) * SLOTS + j]
                if k == 0:
                    kin[zl * SLOTS + j] = block
                else:
                    packz[(k - 1) * SLOTS + j] = block
            if k:
                c = copy(packz.at[pl.ds((k - 1) * SLOTS, SLOTS)],
                         kin.at[pl.ds(zl * SLOTS, SLOTS)], at_z(zt))
                packs.append((k, c))
                goes = pl.when(linked(zl, zt))
                goes(c.start)
                open_sends.append((goes, c))
                owed[id(c)] = (pl.when(linked(wrap(zl - k), zl)), c)

    def make_tile():
        for k, c in packs:
            got(c)
        for j in range(SLOTS):
            p = kept[row * SLOTS + j]
            tile[:, j * BLOCK:(j + 1) * BLOCK] = kin[lax.div(p, RING * OWN) * SLOTS + j]
        kr[y, col] = tile[...]

    hop, rsx, rsz, mid, agz, agx, fwd = {}, {}, {}, {}, {}, {}, {}
    place = [(wrap(y - k), lax.rem(zh + w, 2)) for k, w in CHUNKS]

    def stage_a(i):
        k, w = CHUNKS[i]
        gx.ready(k, w)
        q, h = place[i]
        lhs = xg[q, pl.ds(2 * h, 2)].reshape(PAIR, FEAT)
        out = jnp.dot(lhs, wv[...], preferred_element_type=F32)
        part[i] = out.astype(BF16)
        mine[i] = out
        if not RELAYED[i]:
            for n, k in enumerate((2, 1, 3)):
                rsx[i, n, 0] = push(part.at[i, pl.ds(wrap(x + k) * SUB, SUB)], xin.at[i, n], to_x(k))
            return
        for n, k in enumerate((1, 3)):
            hop[i, n] = push(part.at[i, pl.ds(wrap(x + 2) * SUB + n * HALF, HALF)], hopin.at[i, n], to_x(k))
        for n, k in enumerate((1, 3)):
            lo = (1 - n) * HALF
            rsx[i, n, 0] = push(part.at[i, pl.ds(wrap(x + k) * SUB + lo, HALF)],
                                xin.at[i, n, pl.ds(lo, HALF)], to_x(k))

    def stage_h(i):
        for n, k in enumerate((1, 3)):
            got(hop[i, n])
            rows = pl.ds(wrap(x + k) * SUB + n * HALF, HALF)
            both[i, n] = (mine[i, rows] + hopin[i, n].astype(F32)).astype(BF16)
            rsx[i, n, 1] = push(both.at[i, n], xin.at[i, n, pl.ds(n * HALF, HALF)], to_x(k))

    def stage_b(i):
        own = mine[i, pl.ds(x * SUB, SUB)]
        for n in range(2 if RELAYED[i] else 3):
            for m in range(2 if RELAYED[i] else 1):
                got(rsx[i, n, m])
        if not RELAYED[i]:
            own = own + xin[i, 2].astype(F32)
        total[i] = own + (xin[i, 0].astype(F32) + xin[i, 1].astype(F32))
        c = copy(total.at[i], zin.at[i], at_z(jnp.where(zl < 2, 1, 2)))
        pl.when(outer)(c.start)
        open_sends.append((pl.when(outer), c))
        owed[id(c)] = (pl.when(inner), c)
        rsz[i] = c

    def stage_c(i):
        c = copy(total.at[i, pl.ds(lax.rem(zl, 2) * HALF, HALF)], zhalf.at[i], at_z(3 - zl))
        mid[i] = c
        owed[id(c)] = (pl.when(inner), c)
        open_sends.append((pl.when(inner), c))

        got(rsz[i])

        @pl.when(inner)
        def _():
            total[i] = total[i] + zin[i]
            c.start()

    def stage_d(i):
        h = lax.rem(zl + 1, 2)
        rows = pl.ds(h * HALF, HALF)
        q, g = place[i]
        piece = tg.at[q, g, x, rows]
        base = count[1]
        count[1] += 2
        cs = [copy(piece, piece, at_z(wrap(zl + k)), base + h) for k in (1, 2, 3)]
        agz[i] = []
        for n in (0, 1):
            c = pltpu.make_async_remote_copy(
                src_ref=tg.at[q, g, x, pl.ds(n * HALF, HALF)],
                dst_ref=tg.at[q, g, x, pl.ds(n * HALF, HALF)], send_sem=send_sem.at[0],
                recv_sem=recv_sem.at[base + n], device_id=to_sib, device_id_type=MESH)
            owed[id(c)] = (pl.when(zl != n + 1), c)
            agz[i].append(c)
        for c in cs:
            open_sends.append((pl.when(inner), c))

        got(mid[i])

        @pl.when(inner)
        def _():
            tg[q, g, x, rows] = (total[i, rows] + zhalf[i]).astype(BF16)
            for c in cs:
                c.start()

    def stage_e(i):
        q, g = place[i]
        for c in agz[i]:
            got(c)
        piece = tg.at[q, g, x]
        for k in (1, 3):
            agx[i, k] = push(piece, piece, to_x(k))

    def stage_f(i):
        q, g = place[i]
        for k, lo in ((1, 0), (3, HALF)):
            got(agx[i, k])
            piece = tg.at[q, g, wrap(x - k), pl.ds(lo, HALF)]
            fwd[i, k] = push(piece, piece, to_x(k))

    def stage_g(i):
        for k in (1, 3):
            got(fwd[i, k])
        q, g = place[i]
        lhs = kr[q, pl.ds(2 * g, 2)].reshape(PAIR, KEPT)
        rhs = tg[q, g].reshape(PAIR, FEAT)
        out = lax.dot_general(lhs, rhs, (((0,), (0,)), ((), ())), preferred_element_type=F32)
        done.append(i)
        if len(done) == 1:
            cross_ref[...] = out
        elif len(done) < len(CHUNKS):
            cross_ref[...] += out
        else:
            cross_ref[...] = (cross_ref[...] + out) * INV

    def tile_out():
        make_tile()
        gather["k"] = Gather(kr, tile)
        c = copy(tile, kc.at[col, y], flip)
        pl.when(off_diagonal)(c.start)
        open_sends.append((pl.when(off_diagonal), c))
        owed[id(c)] = (pl.when(off_diagonal), c)
        share.append(c)

        @pl.when(jnp.logical_not(off_diagonal))
        def _():
            kc[x, zl] = tile[...]

    def hand(which, i):
        gather[which].hand(*CHUNKS[i])

    def spread(which):
        gather[which].spread()

    def share_here():
        if share:
            got(share.pop())
        return kc.at[x, zl]

    def share_z(k):
        piece = share_here()
        colz[k] = push(piece, piece, at_z(wrap(zl + k)))

    def share_x(k):
        if k:
            got(colz[k])
            piece = kc.at[x, wrap(zl - k)]
        else:
            piece = share_here()
        for d in (1, 3):
            colx[k, d] = push(piece, piece, to_x(d))

    def share_fwd(h):
        for k, d in ((2 * h, 1), (2 * h + 1, 3)):
            for e in (1, 3):
                got(colx[k, e])
            piece = kc.at[wrap(x - d), wrap(zl - k)]
            colf.append(push(piece, piece, to_x(d)))

    def k_ready():
        for k, w in CHUNKS:
            gather["k"].ready(k, w)

    def gram():
        for c in colf:
            got(c)

        def gram_body(j, carry):
            lhs = kr[:, j].reshape(RING * TOK, KEPT)
            rhs = kc[j].reshape(RING * TOK, KEPT)
            gram_ref[...] += lax.dot_general(lhs, rhs, (((0,), (0,)), ((), ())), preferred_element_type=F32)
            return carry

        gram_ref[...] = jnp.zeros_like(gram_ref)
        lax.fori_loop(0, RING, gram_body, 0)
        gram_ref[...] = gram_ref[...] * INV

    gather, share, colz, colx, colf = {"x": gx}, [], {}, {}, []
    A, H, B, C, D, E, F, G = stage_a, stage_h, stage_b, stage_c, stage_d, stage_e, stage_f, stage_g
    steps = (
        (loads[1 + OWN].wait,), (A, 0), (hand, "x", 1), (hand, "x", 2), (send_packs,), (A, 1),
        (spread, "x"), (B, 0), (A, 2), (tile_out,), (hand, "x", 5), (hand, "x", 6), (B, 1), (A, 5),
        (C, 0), (A, 4), (hand, "x", 7), (H, 5), (B, 2), (A, 7), (D, 0), (spread, "k"), (hand, "x", 3),
        (hand, "k", 3), (H, 4), (hand, "k", 1), (B, 5), (C, 1), (H, 7), (A, 6), (A, 3), (hand, "k", 6),
        (B, 4), (C, 2), (E, 0), (D, 1), (hand, "k", 7), (C, 5), (D, 2), (H, 6), (B, 7), (hand, "k", 5),
        (E, 1), (share_z, 1), (C, 4), (share_x, 0), (F, 0), (share_z, 3), (share_z, 2), (B, 3), (F, 1),
        (E, 2), (hand, "k", 2), (share_x, 1), (C, 7), (D, 4), (D, 5), (share_x, 3), (F, 2),
        (share_fwd, 0), (B, 6), (share_x, 2), (D, 7), (E, 4), (C, 3), (E, 5), (C, 6), (k_ready,),
        (share_fwd, 1), (E, 7), (D, 3), (F, 5), (D, 6), (F, 4), (E, 3), (G, 2), (E, 6), (G, 0), (G, 1),
        (G, 5), (F, 3), (G, 4), (F, 7), (F, 6), (gram,), (G, 3), (G, 7), (G, 6),
    )
    for step, *args in steps:
        step(*args)

    for when, c in tuple(owed.values()):
        when(c.wait_recv)
    for when, c in open_sends:
        when(c.wait_send)


def local(teacher_in, weight, student_in, kept_blocks):
    vmem = pl.BlockSpec(memory_space=pltpu.VMEM)
    hbm = pl.BlockSpec(memory_space=pltpu.HBM)
    n = len(CHUNKS)
    return pl.pallas_call(
        kernel,
        out_shape=(jax.ShapeDtypeStruct((KEPT, KEPT), F32),
                   jax.ShapeDtypeStruct((KEPT, FEAT), F32)),
        in_specs=[pl.BlockSpec(memory_space=pltpu.SMEM), hbm, hbm, hbm],
        out_specs=(vmem, vmem),
        scratch_shapes=[
            pltpu.VMEM((RING, RING, TOK, FEAT), BF16),
            pltpu.VMEM((FEAT, FEAT), BF16),
            pltpu.VMEM((OWN, TOK, BLOCK), BF16),
            pltpu.VMEM((n, PAIR, FEAT), BF16),
            pltpu.VMEM((n, PAIR, FEAT), F32),
            pltpu.VMEM((n, 2, HALF, FEAT), BF16),
            pltpu.VMEM((n, 2, HALF, FEAT), BF16),
            pltpu.VMEM((n, 3, SUB, FEAT), BF16),
            pltpu.VMEM((n, SUB, FEAT), F32),
            pltpu.VMEM((n, SUB, FEAT), F32),
            pltpu.VMEM((n, HALF, FEAT), F32),
            pltpu.VMEM((RING, 2, RING, SUB, FEAT), BF16),
            pltpu.VMEM((3 * SLOTS, TOK, BLOCK), BF16),
            pltpu.VMEM((RING * SLOTS, TOK, BLOCK), BF16),
            pltpu.VMEM((3 * SLOTS, TOK, BLOCK), BF16),
            pltpu.VMEM((RING * SLOTS, TOK, BLOCK), BF16),
            pltpu.VMEM((TOK, KEPT), BF16),
            pltpu.VMEM((RING, RING, TOK, KEPT), BF16),
            pltpu.VMEM((RING, RING, TOK, KEPT), BF16),
            pltpu.SemaphoreType.DMA((2 + OWN,)),
            pltpu.SemaphoreType.DMA((COPIES,)),
            pltpu.SemaphoreType.DMA((COPIES,)),
        ],
        compiler_params=pltpu.CompilerParams(
            collective_id=0, has_side_effects=True, vmem_limit_bytes=VMEM),
        name="gram_cross",
    )(kept_blocks, teacher_in, weight, student_in)


def solution(mesh):
    return jax.shard_map(
        local,
        mesh=mesh,
        in_specs=(
            P(("grp", "col"), "row"),
            P("row", ("grp", "col")),
            P(("grp", "col"), "row"),
            P(),
        ),
        out_specs=(P("row", ("grp", "col")), P("row", ("grp", "col"))),
        check_vma=False,
    )
```
